128 devices in a mesh: visit: 8 (over z, core), patch: 16 (over x, y).
Axes of the slice: x: 4, y: 4, z: 4, core: 2. Of those that a mesh axis runs over, the one named last changes fastest.
Arguments:
- science: bfloat16 [16, 256, 128, 128], P('visit', 'patch'), may hold values from -6 to 6
- tile_ids: int32 [16, 256], P('visit', 'patch'), may hold values from 0 to 255, as said below
- valid: int32 [16, 256], P('visit', 'patch'), may hold values 0 or 1
- weights: bfloat16 [16, 256], P('visit', 'patch'), may hold values from 0.25 to 4
- kernel_weight_terms: bfloat16 [16, 6, 25], P('visit'), may hold values from -30 to 30
- prior_template: float32 [2048, 2048], P(None, 'patch'), may hold values from -6 to 6
- prior_weight: float32 [2048, 2048], P(None, 'patch'), may hold values from 0.5 to 4
Outputs:
- difference: bfloat16 [16, 256, 128, 128], P('visit', 'patch')
The draws below stay inside these ranges and needn't reach their ends.
Inputs may be any that keep to these rules, and one draw needn't show every extreme that they name: `tile_ids`: among the 2 x 16 entries held by one device, at most 4 name tiles of one strip (entry // 16); for each index of visit, one strip receives exactly 4 entries from every device of that index.
All inputs are finite; a program needn't handle non-finite values. No bound on the sum of `valid` on one device may be relied on, other than what follows from the above.
Results may differ from the reference program's by a relative error of at most 0.0071.
Values may be sent and summed in bfloat16 or wider, within the bound.
A program may use at most 128 MiB of HBM per device.

```python
import math
import jax
import jax.numpy as jnp
from jax import lax

TILE = 128
KHALF = 15
NBASIS = 25
NPOLY = 6
SLOTS = 16
VIS_DEV = 2
PT = 16
VISITS = 16
VSLOTS = 256
SKY_H = 2048
SKY_W = 2048
N_VISIT = 8
N_PATCH = 16


def draw_tile_ids(key, part):
    block_len = VIS_DEV * SLOTS
    capacity = 2 * block_len // N_PATCH
    remainder = block_len - capacity

    def device_block(partition_key, busiest):
        pool_key, order_key, tile_key = jax.random.split(partition_key, 3)
        others = (busiest + 1 + jnp.arange((N_PATCH - 1) * capacity, dtype=jnp.int32) // capacity) % N_PATCH
        chosen = jax.random.permutation(pool_key, others)[:remainder]
        owners = jnp.concatenate([jnp.full((capacity,), busiest, jnp.int32), chosen])
        owners = jax.random.permutation(order_key, owners)
        local_index = jax.random.randint(tile_key, (block_len,), 0, PT, dtype=jnp.int32)
        return owners * PT + local_index
    hot_key, block_key = jax.random.split(jax.random.fold_in(key, 11))
    busiest = jax.random.randint(hot_key, (N_VISIT,), 0, N_PATCH, dtype=jnp.int32)
    block_keys = jax.random.split(block_key, N_VISIT * N_PATCH)
    blocks = jax.vmap(device_block)(block_keys, jnp.repeat(busiest, N_PATCH))
    return blocks.reshape(N_VISIT, N_PATCH, VIS_DEV, SLOTS).transpose(0, 2, 1, 3).reshape(VIS_DEV * N_VISIT, SLOTS * N_PATCH)


def plant(drawn, stream_key, least, largest):
    spot = [jax.random.randint(jax.random.fold_in(stream_key, axis), (), 0, length) for axis, length in enumerate(drawn.shape)]
    main_axis = drawn.shape.index(max(drawn.shape))
    next_to = spot[:main_axis] + [(spot[main_axis] + 1) % drawn.shape[main_axis]] + spot[main_axis + 1:]
    return drawn.at[tuple(spot)].set(least).at[tuple(next_to)].set(largest)


def block_scale(key, dims, cuts, low, top_value):
    factor_of = 1.0
    for position, blocks in cuts:
        steps = jax.random.uniform(jax.random.fold_in(jax.random.fold_in(key, 6), position), (blocks,), jnp.float32, low / len(cuts), top_value / len(cuts))
        factor_of = factor_of * jnp.repeat(jnp.exp(steps), dims[position] // blocks).reshape((-1,) + (1,) * (len(dims) - 1 - position))
    return factor_of


def scatter_about(own_key, dims, spread, most, shards=(), kind=jnp.bfloat16):
    values = jax.random.normal(own_key, dims, jnp.float32) * spread
    if len(shards) > 0:
        values = block_scale(own_key, dims, shards, -0.22, 0.18) * values
    return jnp.clip(values, min=-most, max=most).astype(kind)


def setup_inputs(seed: int = 0) -> dict:
    splits = jax.random.split(jax.random.key(seed), 8)
    return {
        "science": scatter_about(splits[0], (VISITS, VSLOTS, TILE, TILE), 1.0, 6.0, ((0, 8), (1, 16))),
        "tile_ids": draw_tile_ids(jax.random.fold_in(splits[7], 71), 0),
        "valid": plant((jax.random.randint(splits[2], (VISITS, VSLOTS), 0, 4) < 3).astype(jnp.int32), jax.random.fold_in(splits[2], 1), 0, 1),
        "weights": jnp.clip(jnp.exp(math.log(4.0) - 2.7725887 * jax.random.uniform(splits[3], (VISITS, VSLOTS), jnp.float32) ** block_scale(splits[3], (VISITS, VSLOTS), ((0, 8), (1, 16)), -0.2, 0.2)), 0.25, 4.0).astype(jnp.bfloat16),
        "kernel_weight_terms": scatter_about(splits[4], (VISITS, NPOLY, NBASIS), 6.0, 30.0, ((0, 8),)),
        "prior_template": scatter_about(splits[5], (SKY_H, SKY_W), 1.0, 6.0, ((1, 16),), jnp.float32),
        "prior_weight": jnp.clip(jnp.exp(math.log(4.0) - 2.0794415 * jax.random.uniform(splits[6], (SKY_H, SKY_W), jnp.float32) ** block_scale(splits[6], (SKY_H, SKY_W), ((1, 16),), -0.2, 0.2)), 0.5, 4.0),
    }


SIGMAS = (1.5, 3.0, 5.0, 7.0)
DEGREES = (4, 2, 1, 0)


def profile_table():
    offsets = jnp.arange(2 * KHALF + 1, dtype=jnp.float32) - KHALF
    profiles = []
    for gauss_sigma, poly_degree in zip(SIGMAS, DEGREES):
        scaled = offsets / gauss_sigma
        envelope = jnp.exp(-0.5 * scaled * scaled)
        for exponent in range(poly_degree + 1):
            shaped = envelope * scaled ** exponent
            profiles.append(shaped / jnp.sum(jnp.abs(shaped)))
    return jnp.stack(profiles).astype(jnp.bfloat16)


def band_tables(profiles, count):
    target = jnp.arange(count, dtype=jnp.int32)[:, None]
    source = jnp.arange(count + 2 * KHALF, dtype=jnp.int32)[None, :]
    taps_index = jnp.arange(2 * KHALF + 1, dtype=jnp.int32)
    selector = ((source - target)[:, :, None] == taps_index[None, None, :]).astype(jnp.float32)
    return jnp.einsum("abu,pu->pab", selector, profiles.astype(jnp.float32)).astype(jnp.bfloat16)


def basis_images(padded):
    height = padded.shape[0]
    tiles_count = height // TILE
    profiles = profile_table()
    profile_count = profiles.shape[0]
    across_tiles = band_tables(profiles, TILE)
    column_matrix = jnp.transpose(across_tiles, (2, 0, 1)).reshape(TILE + 2 * KHALF, profile_count * TILE)
    smoothed = jnp.dot(padded, column_matrix, preferred_element_type=jnp.float32).astype(jnp.bfloat16)
    extended = jnp.pad(smoothed, ((KHALF, TILE - KHALF), (0, 0)))
    upper_rows = extended[:height].reshape(tiles_count, TILE, profile_count * TILE)
    lower_rows = extended[TILE:height + TILE].reshape(tiles_count, TILE, profile_count * TILE)[:, :2 * KHALF]
    windows = jnp.concatenate([upper_rows, lower_rows], axis=1)
    images = []
    profile_offset = 0
    for poly_degree in DEGREES:
        for row_exponent in range(poly_degree + 1):
            column_count = poly_degree - row_exponent + 1
            window_columns = windows[:, :, profile_offset * TILE:(profile_offset + column_count) * TILE]
            final_output = jnp.einsum("uh,vhp->vup", across_tiles[profile_offset + row_exponent].astype(jnp.float32), window_columns.astype(jnp.float32))
            images.append(jnp.transpose(final_output.reshape(tiles_count, TILE, column_count, TILE), (0, 2, 1, 3)))
        profile_offset = profile_offset + poly_degree + 1
    stacked = jnp.concatenate(images, axis=1).astype(jnp.bfloat16)
    return stacked.reshape(tiles_count, stacked.shape[1], TILE * TILE)


def poly_terms(owner_index, tile_index, sky_height, sky_width):
    pixel_axis = jnp.arange(TILE, dtype=jnp.float32)
    xcoord = (owner_index[:, None, None] * TILE + pixel_axis[None, None, :] + 0.5) / sky_width * 2.0 - 1.0
    ycoord = (tile_index[:, None, None] * TILE + pixel_axis[None, :, None] + 0.5) / sky_height * 2.0 - 1.0
    xcoord = jnp.broadcast_to(xcoord, (owner_index.shape[0], TILE, TILE))
    ycoord = jnp.broadcast_to(ycoord, (owner_index.shape[0], TILE, TILE))
    monomials = [jnp.ones_like(xcoord), xcoord, ycoord, xcoord * xcoord, xcoord * ycoord, ycoord * ycoord]
    return jnp.stack(monomials, axis=1).reshape(owner_index.shape[0], NPOLY, TILE * TILE)


def reference(science, tile_ids, valid, weights, kernel_weight_terms, prior_template, prior_weight):
    tile_total = PT * N_PATCH
    pixel_total = TILE * TILE

    def accumulate(carry, operands):
        numerator, weight_sum = carry
        visit_pixels, visit_ids, visit_valid, visit_weights = operands
        weighted = visit_weights.astype(jnp.float32) * visit_valid.astype(jnp.float32)
        contrib = weighted[:, None] * visit_pixels.reshape(VSLOTS, pixel_total).astype(jnp.float32)
        numerator = numerator + jax.ops.segment_sum(contrib, visit_ids, num_segments=tile_total)
        weight_sum = weight_sum + jax.ops.segment_sum(weighted, visit_ids, num_segments=tile_total)
        return (numerator, weight_sum), None

    starting = (jnp.zeros((tile_total, pixel_total), jnp.float32), jnp.zeros((tile_total,), jnp.float32))
    (numerator, weight_sum), unused = lax.scan(accumulate, starting, (science, tile_ids, valid, weights))
    sky_num = numerator.reshape(N_PATCH, PT, TILE, TILE).transpose(1, 2, 0, 3).reshape(PT * TILE, N_PATCH * TILE)
    sky_weight = jnp.repeat(jnp.repeat(weight_sum.reshape(N_PATCH, PT).T, TILE, axis=0), TILE, axis=1)
    template = ((prior_weight * prior_template + sky_num) / (prior_weight + sky_weight)).astype(jnp.bfloat16)
    padded_sky = jnp.pad(template, ((0, 0), (KHALF, KHALF)))

    def strip_basis(owner):
        return basis_images(lax.dynamic_slice_in_dim(padded_sky, owner * TILE, TILE + 2 * KHALF, 1))

    all_basis = lax.map(strip_basis, jnp.arange(N_PATCH, dtype=jnp.int32))
    all_basis = all_basis.reshape(tile_total, NBASIS, pixel_total).astype(jnp.float32)

    def visit_difference(operands):
        visit_pixels, visit_ids, visit_valid, visit_coeffs = operands
        combined = jnp.einsum("mk,nkp->nmp", visit_coeffs.astype(jnp.float32), all_basis)

        def slot_block(block_ops):
            block_pixels, block_ids, block_valid = block_ops
            chosen = jnp.take(combined, block_ids, axis=0)
            monomials = poly_terms((block_ids // PT).astype(jnp.float32), (block_ids % PT).astype(jnp.float32), PT * TILE, N_PATCH * TILE)
            matched = jnp.sum(monomials * chosen, axis=1)
            residue = block_pixels.reshape(SLOTS, pixel_total).astype(jnp.float32) - matched
            return (block_valid.astype(jnp.float32)[:, None] * residue).astype(jnp.bfloat16)

        diffs = lax.map(slot_block, (visit_pixels.reshape(N_PATCH, SLOTS, TILE, TILE), visit_ids.reshape(N_PATCH, SLOTS), visit_valid.reshape(N_PATCH, SLOTS)))
        return diffs.reshape(VSLOTS, TILE, TILE)

    return lax.map(visit_difference, (science, tile_ids, valid, kernel_weight_terms))
```

```python
import math

import jax
import jax.numpy as jnp
import ml_dtypes
import numpy as np
from jax import lax
from jax.experimental import pallas as pl
from jax.experimental.pallas import tpu as pltpu
from jax.sharding import PartitionSpec as P

TILE = 128
KHALF = 15
HALO = 16
SPAN = TILE + 2 * HALO
SIGMAS = (1.5, 3.0, 5.0, 7.0)
DEGREES = (4, 2, 1, 0)
NPROF = 11
NBASIS = 25
NPOLY = 6
PT = 16
SKY = 2048
VIS = 2
GROUP = 3 * VIS * TILE
BLOCK = 4


def profile_table():
    u = np.arange(-KHALF, KHALF + 1, dtype=np.float32)
    rows = []
    for sigma, degree in zip(SIGMAS, DEGREES):
        scaled = u / np.float32(sigma)
        envelope = np.exp(np.float32(-0.5) * scaled * scaled)
        for power in range(degree + 1):
            shaped = envelope * scaled**power
            rows.append(shaped / np.sum(np.abs(shaped)))
    return np.stack(rows).astype(np.float32)


def band_constants():
    profiles = profile_table()
    target = np.arange(TILE)

    def band(source):
        taps = source[:, None] - target[None, :] + KHALF
        inside = (taps >= 0) & (taps <= 2 * KHALF)
        return np.where(inside[None], profiles[:, np.clip(taps, 0, 2 * KHALF)], 0.0)

    columns = np.concatenate(
        [np.arange(TILE), np.arange(-HALO, 0), np.arange(TILE, TILE + HALO)]
    )
    across = band(columns).astype(ml_dtypes.bfloat16)
    down = band(np.arange(-HALO, TILE + HALO)).transpose(2, 0, 1)
    down = down.reshape(TILE, NPROF * SPAN).astype(ml_dtypes.bfloat16)
    return across, down


def basis_order():
    order, start = [], 0
    for degree in DEGREES:
        for j in range(degree + 1):
            order.append((start + j, [start + i for i in range(degree - j + 1)]))
        start += degree + 1
    return order


def build_weights(strip, kw_ref, across_ref, w_ref):
    lane = lax.broadcasted_iota(jnp.int32, (1, TILE), 1) + strip * TILE
    x = (lane.astype(jnp.float32) + 0.5) / SKY * 2.0 - 1.0
    xx = x * x
    k = 0
    for j, sources in basis_order():
        for v in range(VIS):
            sums = [None, None, None]
            for n, source in enumerate(sources):
                c = [kw_ref[v, m, k + n] for m in range(NPOLY)]
                rows = (c[0] + c[1] * x + c[3] * xx, c[2] + c[4] * x, c[5])
                image = across_ref[source].astype(jnp.float32)
                for b in range(3):
                    term = rows[b] * image
                    sums[b] = term if sums[b] is None else sums[b] + term
            for b in range(3):
                at = (b * VIS + v) * TILE
                w_ref[j, :, at : at + TILE] = sums[b].astype(jnp.bfloat16)
        k += len(sources)


def match_tiles(block, padded_ref, down_ref, w_ref, h_ref, store):
    rows = BLOCK * TILE + 2 * HALO
    top = pl.multiple_of(block * (BLOCK * TILE), 16)

    @pl.loop(0, NPROF)
    def _(j):
        h_ref[j] = jnp.dot(
            padded_ref[pl.ds(top, rows), :SPAN], w_ref[j], preferred_element_type=jnp.float32
        ).astype(jnp.bfloat16)

    @pl.loop(0, BLOCK)
    def _(n):
        begin = pl.multiple_of(n * TILE, 16)
        tile = block * BLOCK + n
        window = h_ref[:, pl.ds(begin, SPAN), :].reshape(NPROF * SPAN, GROUP)
        line = lax.broadcasted_iota(jnp.int32, (TILE, 1), 0) + tile * TILE
        y = (line.astype(jnp.float32) + 0.5) / SKY * 2.0 - 1.0
        total = jnp.dot(down_ref[...], window, preferred_element_type=jnp.float32)
        half = VIS * TILE
        both = total[:, :half] + y * total[:, half : 2 * half] + (y * y) * total[:, 2 * half :]
        for v in range(VIS):
            store(v, tile, both[:, v * TILE : (v + 1) * TILE].astype(jnp.bfloat16))


def match_kernel(strip_ref, kw_ref, padded_ref, across_ref, down_ref, out_ref, w_ref, h_ref):
    build_weights(strip_ref[0], kw_ref, across_ref, w_ref)

    def store(v, tile, value):
        out_ref[v * PT + tile] = value

    @pl.loop(0, PT // BLOCK)
    def _(block):
        match_tiles(block, padded_ref, down_ref, w_ref, h_ref, store)


def match(strip, kw, padded):
    across, down = band_constants()
    vmem = pl.BlockSpec(memory_space=pltpu.VMEM)
    smem = pl.BlockSpec(memory_space=pltpu.SMEM)
    return pl.pallas_call(
        match_kernel,
        out_shape=jax.ShapeDtypeStruct((VIS * PT, TILE, TILE), jnp.bfloat16),
        in_specs=[smem, smem, vmem, vmem, vmem],
        out_specs=vmem,
        scratch_shapes=[
            pltpu.VMEM((NPROF, SPAN, GROUP), jnp.bfloat16),
            pltpu.VMEM((NPROF, BLOCK * TILE + 2 * HALO, GROUP), jnp.bfloat16),
        ],
        compiler_params=pltpu.CompilerParams(vmem_limit_bytes=48 << 20),
    )(strip, kw, padded, jnp.asarray(across), jnp.asarray(down))


def body(science, tile_ids, valid, weights, kernel_weight_terms, prior_template, prior_weight):
    slots = tile_ids.size
    owners = lax.axis_size("patch")
    capacity = 4
    length = owners * capacity
    ids = tile_ids.reshape(slots)
    flag = valid.reshape(slots)
    destination = ids // PT
    local_tile = ids % PT
    visit_local = jnp.arange(slots, dtype=jnp.int32) // tile_ids.shape[1]
    same = destination[:, None] == destination[None, :]
    before = jnp.arange(slots)[:, None] > jnp.arange(slots)[None, :]
    ranking = jnp.sum((same & before).astype(jnp.int32), axis=1)
    position = destination * capacity + ranking
    placed = position[None, :] == jnp.arange(length, dtype=jnp.int32)[:, None]
    occupied = jnp.any(placed, axis=1)
    source_slot = jnp.sum(jnp.where(placed, jnp.arange(slots, dtype=jnp.int32)[None, :], 0), axis=1)
    pixels = science.reshape(slots, TILE, TILE)
    outgoing = jnp.where(
        occupied[:, None, None], jnp.take(pixels, source_slot, axis=0), jnp.zeros((), jnp.bfloat16)
    )
    weighted = weights.reshape(slots).astype(jnp.float32) * flag.astype(jnp.float32)
    details = jnp.stack(
        [weighted, local_tile.astype(jnp.float32), visit_local.astype(jnp.float32)], axis=1
    )
    details = jnp.where(occupied[:, None], jnp.take(details, source_slot, axis=0), 0.0)
    arrived = lax.all_to_all(outgoing, "patch", split_axis=0, concat_axis=0, tiled=True)
    arrived_details = lax.all_to_all(
        details.astype(jnp.bfloat16), "patch", split_axis=0, concat_axis=0, tiled=True
    )
    arrived_weight = arrived_details[:, 0]
    arrived_tile = arrived_details[:, 1].astype(jnp.int32)
    arrived_visit = arrived_details[:, 2].astype(jnp.int32)
    tile_match = arrived_tile[None, :] == jnp.arange(PT, dtype=jnp.int32)[:, None]
    spread = jnp.where(tile_match, arrived_weight[None, :], jnp.zeros((), jnp.bfloat16))
    numerator = jnp.dot(
        spread, arrived.reshape(length, TILE * TILE), preferred_element_type=jnp.float32
    ).reshape(PT * TILE, TILE)
    weight_rows = jnp.repeat(jnp.sum(spread.astype(jnp.float32), axis=1), TILE)
    total, total_weight = lax.psum((numerator, weight_rows), "visit")
    template = (
        (prior_weight * prior_template + total) / (prior_weight + total_weight[:, None])
    ).astype(jnp.bfloat16)
    up = [(i, i + 1) for i in range(owners - 1)]
    down = [(j, i) for i, j in up]
    left = lax.ppermute(template[:, TILE - HALO :], "patch", up)
    right = lax.ppermute(template[:, :HALO], "patch", down)
    padded = jnp.pad(
        jnp.concatenate([template, left, right], axis=1), ((HALO, HALO), (0, 2 * TILE - SPAN))
    )
    strip = lax.axis_index("patch").astype(jnp.int32).reshape(1)
    matched = match(strip, kernel_weight_terms.astype(jnp.float32), padded)
    chosen = jnp.take(matched, arrived_visit * PT + arrived_tile, axis=0)
    returned = lax.all_to_all(chosen, "patch", split_axis=0, concat_axis=0, tiled=True)
    result = (
        pixels.astype(jnp.float32) - jnp.take(returned, position, axis=0).astype(jnp.float32)
    ) * flag.astype(jnp.float32)[:, None, None]
    return result.astype(jnp.bfloat16).reshape(science.shape)


def solution(mesh):
    placed = (
        P("visit", "patch", None, None),
        P("visit", "patch"),
        P("visit", "patch"),
        P("visit", "patch"),
        P("visit", None, None),
        P(None, "patch"),
        P(None, "patch"),
    )
    return jax.shard_map(
        body, mesh=mesh, in_specs=placed, out_specs=P("visit", "patch", None, None), check_vma=False
    )
```

```python
import jax
import jax.numpy as jnp
import ml_dtypes
import numpy as np
from jax import lax
from jax.experimental import pallas as pl
from jax.experimental.pallas import tpu as pltpu
from jax.sharding import PartitionSpec as P

TILE = 128
KHALF = 15
HALO = 16
SPAN = TILE + 2 * HALO
SIGMAS = (1.5, 3.0, 5.0, 7.0)
DEGREES = (4, 2, 1, 0)
NPROF = 11
NBASIS = 25
NPOLY = 6
PT = 16
SKY = 2048
VIS = 2
GROUP = 3 * VIS * TILE
BLOCK = 4
OWNERS = 16
VISITORS = 8
CAP = 4
ROWS = TILE + 8
MESH = pl.DeviceIdType.MESH


def profile_table():
    u = np.arange(-KHALF, KHALF + 1, dtype=np.float32)
    rows = []
    for sigma, degree in zip(SIGMAS, DEGREES):
        scaled = u / np.float32(sigma)
        envelope = np.exp(np.float32(-0.5) * scaled * scaled)
        for power in range(degree + 1):
            shaped = envelope * scaled**power
            rows.append(shaped / np.sum(np.abs(shaped)))
    return np.stack(rows).astype(np.float32)


def band_constants():
    profiles = profile_table()
    target = np.arange(TILE)

    def band(source):
        taps = source[:, None] - target[None, :] + KHALF
        inside = (taps >= 0) & (taps <= 2 * KHALF)
        return np.where(inside[None], profiles[:, np.clip(taps, 0, 2 * KHALF)], 0.0)

    columns = np.concatenate(
        [np.arange(TILE), np.arange(-HALO, 0), np.arange(TILE, TILE + HALO)]
    )
    across = band(columns).astype(ml_dtypes.bfloat16)
    down = band(np.arange(-HALO, TILE + HALO)).transpose(2, 0, 1)
    down = down.reshape(TILE, NPROF * SPAN).astype(ml_dtypes.bfloat16)
    return across, down


def basis_order():
    order, start = [], 0
    for degree in DEGREES:
        for j in range(degree + 1):
            order.append((start + j, [start + i for i in range(degree - j + 1)]))
        start += degree + 1
    return order


def build_weights(strip, kw_ref, across_ref, w_ref):
    lane = lax.broadcasted_iota(jnp.int32, (1, TILE), 1) + strip * TILE
    x = (lane.astype(jnp.float32) + 0.5) / SKY * 2.0 - 1.0
    xx = x * x
    k = 0
    for j, sources in basis_order():
        for v in range(VIS):
            sums = [None, None, None]
            for n, source in enumerate(sources):
                c = [kw_ref[v, m, k + n] for m in range(NPOLY)]
                rows = (c[0] + c[1] * x + c[3] * xx, c[2] + c[4] * x, c[5])
                image = across_ref[source].astype(jnp.float32)
                for b in range(3):
                    term = rows[b] * image
                    sums[b] = term if sums[b] is None else sums[b] + term
            for b in range(3):
                at = (b * VIS + v) * TILE
                w_ref[j, :, at : at + TILE] = sums[b].astype(jnp.bfloat16)
        k += len(sources)


def match_tiles(block, padded_ref, down_ref, w_ref, h_ref, store):
    rows = BLOCK * TILE + 2 * HALO
    top = pl.multiple_of(block * (BLOCK * TILE), 16)

    @pl.loop(0, NPROF)
    def _(j):
        h_ref[j] = jnp.dot(
            padded_ref[pl.ds(top, rows), :SPAN], w_ref[j], preferred_element_type=jnp.float32
        ).astype(jnp.bfloat16)

    @pl.loop(0, BLOCK)
    def _(n):
        begin = pl.multiple_of(n * TILE, 16)
        tile = block * BLOCK + n
        window = h_ref[:, pl.ds(begin, SPAN), :].reshape(NPROF * SPAN, GROUP)
        line = lax.broadcasted_iota(jnp.int32, (TILE, 1), 0) + tile * TILE
        y = (line.astype(jnp.float32) + 0.5) / SKY * 2.0 - 1.0
        total = jnp.dot(down_ref[...], window, preferred_element_type=jnp.float32)
        half = VIS * TILE
        both = total[:, :half] + y * total[:, half : 2 * half] + (y * y) * total[:, 2 * half :]
        for v in range(VIS):
            store(v, tile, both[:, v * TILE : (v + 1) * TILE].astype(jnp.bfloat16))


def remote(src, dst, send, recv, visit, patch):
    return pltpu.make_async_remote_copy(
        src_ref=src,
        dst_ref=dst,
        send_sem=send,
        recv_sem=recv,
        device_id={"visit": visit, "patch": patch},
        device_id_type=MESH,
    )


def kernel(
    source_ref, position_ref, flag_ref, kw_ref, science_ref, label_ref, weight_ref,
    prior_ref, prior_weight_ref, across_ref, down_ref, out_ref,
    w_ref, h_ref, padded_ref, matched_ref, outgoing_ref, arrived_ref, returned_ref,
    acc_ref, pair_ref, ring_ref, side_ref, edge_ref, prior_vmem, labels_vmem, weights_vmem,
    labels_ref, weights_ref, coef_ref,
    local_sem, label_send, label_recv, weight_send, weight_recv, tile_send, tile_recv,
    pair_sem, ring_send, ring_recv, side_send, side_recv, strip_send, strip_recv,
    edge_send, edge_recv, back_send, back_recv,
):
    visit = lax.axis_index("visit")
    me = lax.axis_index("patch")
    z, core = visit // 2, visit % 2
    own = core * 4 + z

    def peer(k):
        return lax.rem(me + k, OWNERS)

    def origin(k):
        return lax.rem(me + OWNERS - k, OWNERS)

    def other(k):
        to = lax.rem(visit + k, VISITORS)
        return to, (to % 2) * 4 + to // 2

    def earlier(k):
        to = lax.rem(visit + VISITORS - k, VISITORS)
        return (to % 2) * 4 + to // 2

    prior_copies = [
        pltpu.make_async_copy(
            ref.at[pl.ds(pl.multiple_of(own * 256, 256), 256), :],
            prior_vmem.at[n],
            local_sem.at[n],
        )
        for n, ref in enumerate((prior_ref, prior_weight_ref))
    ]
    for copy in prior_copies:
        copy.start()

    barrier = pltpu.get_barrier_semaphore()

    @pl.loop(1, OWNERS)
    def _(k):
        pl.semaphore_signal(
            barrier, inc=1, device_id={"visit": visit, "patch": peer(k)}, device_id_type=MESH
        )

    @pl.loop(1, VISITORS)
    def _(k):
        pl.semaphore_signal(
            barrier, inc=1, device_id={"visit": other(k)[0], "patch": me}, device_id_type=MESH
        )

    pl.semaphore_wait(barrier, OWNERS + VISITORS - 2)

    def label_copy(k):
        to = peer(k)
        return remote(
            label_ref.at[to], labels_vmem.at[me], label_send.at[k], label_recv.at[me], visit, to
        )

    def weight_copy(k):
        to = peer(k)
        return remote(
            weight_ref.at[to], weights_vmem.at[me], weight_send.at[k], weight_recv.at[me], visit, to
        )

    def label_wait(k):
        to = origin(k)
        remote(
            label_ref.at[to], labels_vmem.at[to], label_send.at[k], label_recv.at[to], visit, to
        ).wait_recv()
        remote(
            weight_ref.at[to], weights_vmem.at[to], weight_send.at[k], weight_recv.at[to], visit, to
        ).wait_recv()

    def tile_copy(k):
        to = peer(k)
        return remote(
            outgoing_ref.at[to], arrived_ref.at[me], tile_send.at[k], tile_recv.at[me], visit, to
        )

    def tile_wait(k):
        to = origin(k)
        remote(
            outgoing_ref.at[to], arrived_ref.at[to], tile_send.at[k], tile_recv.at[to], visit, to
        ).wait_recv()

    @pl.loop(1, OWNERS)
    def _(k):
        label_copy(k).start()
        weight_copy(k).start()

    def pack(to, target, at):
        for c in range(CAP):
            target[at, c] = science_ref[source_ref[to * CAP + c]]

    @pl.loop(1, OWNERS)
    def _(k):
        pack(peer(k), outgoing_ref, peer(k))
        tile_copy(k).start()

    pack(me, arrived_ref, me)
    labels_vmem[me] = label_ref[me]
    weights_vmem[me] = weight_ref[me]
    build_weights(me, kw_ref, across_ref, w_ref)

    @pl.loop(1, OWNERS)
    def _(k):
        label_wait(k)

    scalars = [
        pltpu.make_async_copy(labels_vmem, labels_ref, local_sem.at[2]),
        pltpu.make_async_copy(weights_vmem, weights_ref, local_sem.at[3]),
    ]
    for copy in scalars:
        copy.start()
    acc_ref[...] = jnp.zeros_like(acc_ref)
    padded_ref[...] = jnp.zeros_like(padded_ref)
    for copy in scalars:
        copy.wait()

    @pl.loop(0, OWNERS)
    def _(k):
        at = origin(k)

        @pl.when(k > 0)
        def _():
            tile_wait(k)

        for t in range(PT):
            total = 0.0
            for c in range(CAP):
                value = jnp.where(labels_ref[at, 0, c] % PT == t, weights_ref[at, 0, c], 0.0)
                coef_ref[t * CAP + c] = value
                total = total + value
            acc_ref[t, TILE:ROWS, :] += jnp.full((ROWS - TILE, TILE), total, jnp.float32)

        @pl.loop(0, TILE // 32)
        def _(part):
            rows = pl.ds(pl.multiple_of(part * 32, 32), 32)
            slots = [arrived_ref[at, c, rows, :].astype(jnp.float32) for c in range(CAP)]
            for t in range(PT):
                value = acc_ref[t, rows, :]
                for c in range(CAP):
                    value = value + coef_ref[t * CAP + c] * slots[c]
                acc_ref[t, rows, :] = value

    pair = remote(
        acc_ref.at[pl.ds((1 - core) * 8, 8)],
        pair_ref,
        pair_sem.at[0],
        pair_sem.at[1],
        z * 2 + 1 - core,
        me,
    )
    pair.start()
    pair.wait_recv()

    def ring_copy(k):
        to = lax.rem(z + k, 4)
        return remote(
            acc_ref.at[pl.ds(core * 8 + to * 2, 2)],
            ring_ref.at[k - 1],
            ring_send.at[k],
            ring_recv.at[k],
            to * 2 + core,
            me,
        )

    for k in (1, 2, 3, 0):
        to = lax.rem(z + k, 4)
        for n in range(2):
            acc_ref[core * 8 + to * 2 + n] += pair_ref[to * 2 + n]
        if k > 0:
            ring_copy(k).start()
    for copy in prior_copies:
        copy.wait()
    for k in (1, 2, 3):
        ring_copy(k).wait_recv()
    for n in range(2):
        total = acc_ref[own * 2 + n]
        for k in range(3):
            total = total + ring_ref[k, n]
        rows = pl.ds(n * TILE, TILE)
        weight = prior_vmem[1, rows, :]
        template = (weight * prior_vmem[0, rows, :] + total[:TILE]) / (
            weight + total[TILE : TILE + 1]
        )
        at = pl.multiple_of(HALO + own * 256 + n * TILE, 16)
        padded_ref[pl.ds(at, TILE), :TILE] = template.astype(jnp.bfloat16)

    def strip_rows(owner):
        return padded_ref.at[
            pl.ds(pl.multiple_of(HALO + owner * 256, 16), 256), pl.ds(0, TILE)
        ]

    def side_copy(n):
        to = peer(1) if n == 0 else origin(1)
        return remote(
            strip_rows(own), side_ref.at[n], side_send.at[n], side_recv.at[n], visit, to
        )

    for n in range(2):
        side_copy(n).start()

    def strip_copy(k):
        return remote(
            strip_rows(own), strip_rows(own), strip_send.at[k], strip_recv.at[k], other(k)[0], me
        )

    def strip_wait(k):
        at = earlier(k)
        remote(
            strip_rows(at), strip_rows(at), strip_send.at[k], strip_recv.at[k], other(k)[0], me
        ).wait_recv()

    @pl.loop(1, VISITORS)
    def _(k):
        strip_copy(k).start()

    for n in range(2):
        side_copy(n).wait_recv()
    lane = lax.broadcasted_iota(jnp.int32, (64, TILE), 1)
    packed = jnp.zeros((64, TILE), jnp.float32)
    for g in range(4):
        rows = pl.ds(64 * g, 64)
        left = pltpu.roll(side_ref[0, rows, :].astype(jnp.float32), (32 * g + HALO) % TILE, 1)
        right = pltpu.roll(side_ref[1, rows, :].astype(jnp.float32), (32 * g + HALO) % TILE, 1)
        is_left = (lane >= 32 * g) & (lane < 32 * g + HALO) & (me > 0)
        is_right = (lane >= 32 * g + HALO) & (lane < 32 * g + 2 * HALO) & (me < OWNERS - 1)
        packed = jnp.where(is_left, left, jnp.where(is_right, right, packed))
    edge_ref[own] = packed.astype(jnp.bfloat16)

    def edge_copy(k):
        return remote(
            edge_ref.at[own], edge_ref.at[own], edge_send.at[k], edge_recv.at[k], other(k)[0], me
        )

    def edge_wait(k):
        at = earlier(k)
        remote(
            edge_ref.at[at], edge_ref.at[at], edge_send.at[k], edge_recv.at[k], other(k)[0], me
        ).wait_recv()

    @pl.loop(1, VISITORS)
    def _(k):
        edge_copy(k).start()

    @pl.loop(1, VISITORS)
    def _(k):
        strip_wait(k)
        edge_wait(k)

    @pl.loop(0, VISITORS)
    def _(owner):
        block = edge_ref[owner].astype(jnp.float32)
        for g in range(4):
            at = pl.multiple_of(HALO + owner * 256 + 64 * g, 16)
            moved = pltpu.roll(block, (TILE - 32 * g) % TILE, 1) if g else block
            moved = jnp.where(lane < 2 * HALO, moved, 0.0)
            padded_ref[pl.ds(at, 64), TILE : 2 * TILE] = moved.astype(jnp.bfloat16)

    def store(v, tile, value):
        matched_ref[v * PT + tile] = value

    @pl.loop(0, PT // BLOCK)
    def _(block):
        match_tiles(block, padded_ref, down_ref, w_ref, h_ref, store)

    @pl.loop(1, OWNERS)
    def _(k):
        tile_copy(k).wait_send()

    def back_copy(k):
        to = peer(k)
        return remote(
            outgoing_ref.at[to], returned_ref.at[me], back_send.at[k], back_recv.at[me], visit, to
        )

    def back_wait(k):
        to = origin(k)
        remote(
            outgoing_ref.at[to], returned_ref.at[to], back_send.at[k], back_recv.at[to], visit, to
        ).wait_recv()

    @pl.loop(1, OWNERS)
    def _(k):
        to = peer(k)
        for c in range(CAP):
            outgoing_ref[to, c] = matched_ref[labels_ref[to, 0, c]]
        back_copy(k).start()

    for c in range(CAP):
        returned_ref[me, c] = matched_ref[labels_ref[me, 0, c]]

    @pl.loop(1, OWNERS)
    def _(k):
        back_wait(k)

    @pl.loop(0, VIS * PT)
    def _(n):
        at = position_ref[n]
        value = science_ref[n].astype(jnp.float32) - returned_ref[at // CAP, at % CAP].astype(
            jnp.float32
        )
        out_ref[n] = (value * flag_ref[n]).astype(jnp.bfloat16)

    pair.wait_send()
    for k in (1, 2, 3):
        ring_copy(k).wait_send()
    for n in range(2):
        side_copy(n).wait_send()

    @pl.loop(1, VISITORS)
    def _(k):
        strip_copy(k).wait_send()
        edge_copy(k).wait_send()

    @pl.loop(1, OWNERS)
    def _(k):
        label_copy(k).wait_send()
        weight_copy(k).wait_send()
        back_copy(k).wait_send()


def body(science, tile_ids, valid, weights, kernel_weight_terms, prior_template, prior_weight):
    slots = tile_ids.size
    length = OWNERS * CAP
    ids = tile_ids.reshape(slots)
    flag = valid.reshape(slots).astype(jnp.float32)
    destination = ids // PT
    order = jnp.arange(slots, dtype=jnp.int32)
    label = (order // tile_ids.shape[1]) * PT + ids % PT
    same = (destination[:, None] == destination[None, :]) & (order[:, None] > order[None, :])
    position = destination * CAP + jnp.sum(same.astype(jnp.int32), axis=1)
    placed = position[None, :] == jnp.arange(length, dtype=jnp.int32)[:, None]
    source = jnp.sum(jnp.where(placed, order[None, :], 0), axis=1)
    weighted = weights.reshape(slots).astype(jnp.float32) * flag
    spread = ((0, 0), (0, 0), (0, TILE - CAP))
    labels = jnp.sum(jnp.where(placed, label[None, :], 0), axis=1).reshape(OWNERS, 1, CAP)
    weight = jnp.sum(jnp.where(placed, weighted[None, :], 0.0), axis=1).reshape(OWNERS, 1, CAP)
    across, down = band_constants()
    vmem = pl.BlockSpec(memory_space=pltpu.VMEM)
    smem = pl.BlockSpec(memory_space=pltpu.SMEM)
    hbm = pl.BlockSpec(memory_space=pl.ANY)
    dma = pltpu.SemaphoreType.DMA
    result = pl.pallas_call(
        kernel,
        out_shape=jax.ShapeDtypeStruct((slots, TILE, TILE), jnp.bfloat16),
        in_specs=[smem, smem, smem, smem, vmem, vmem, vmem, hbm, hbm, vmem, vmem],
        out_specs=vmem,
        scratch_shapes=[
            pltpu.VMEM((NPROF, SPAN, GROUP), jnp.bfloat16),
            pltpu.VMEM((NPROF, BLOCK * TILE + 2 * HALO, GROUP), jnp.bfloat16),
            pltpu.VMEM((SKY + 2 * HALO, 2 * TILE), jnp.bfloat16),
            pltpu.VMEM((VIS * PT, TILE, TILE), jnp.bfloat16),
            pltpu.VMEM((OWNERS, CAP, TILE, TILE), jnp.bfloat16),
            pltpu.VMEM((OWNERS, CAP, TILE, TILE), jnp.bfloat16),
            pltpu.VMEM((OWNERS, CAP, TILE, TILE), jnp.bfloat16),
            pltpu.VMEM((PT, ROWS, TILE), jnp.float32),
            pltpu.VMEM((PT // 2, ROWS, TILE), jnp.float32),
            pltpu.VMEM((3, 2, ROWS, TILE), jnp.float32),
            pltpu.VMEM((2, 2 * TILE, TILE), jnp.bfloat16),
            pltpu.VMEM((VISITORS, 64, TILE), jnp.bfloat16),
            pltpu.VMEM((2, 2 * TILE, TILE), jnp.float32),
            pltpu.VMEM((OWNERS, 1, TILE), jnp.int32),
            pltpu.VMEM((OWNERS, 1, TILE), jnp.float32),
            pltpu.SMEM((OWNERS, 1, TILE), jnp.int32),
            pltpu.SMEM((OWNERS, 1, TILE), jnp.float32),
            pltpu.SMEM((PT * CAP,), jnp.float32),
            dma((4,)),
            dma((OWNERS,)),
            dma((OWNERS,)),
            dma((OWNERS,)),
            dma((OWNERS,)),
            dma((OWNERS,)),
            dma((OWNERS,)),
            dma((2,)),
            dma((4,)),
            dma((4,)),
            dma((2,)),
            dma((2,)),
            dma((VISITORS,)),
            dma((VISITORS,)),
            dma((VISITORS,)),
            dma((VISITORS,)),
            dma((OWNERS,)),
            dma((OWNERS,)),
        ],
        compiler_params=pltpu.CompilerParams(
            vmem_limit_bytes=56 << 20, collective_id=0, has_side_effects=True
        ),
    )(
        source,
        position,
        flag,
        kernel_weight_terms.astype(jnp.float32),
        science.reshape(slots, TILE, TILE),
        jnp.pad(labels, spread),
        jnp.pad(weight, spread),
        prior_template,
        prior_weight,
        jnp.asarray(across),
        jnp.asarray(down),
    )
    return result.reshape(science.shape)


def solution(mesh):
    placed = (
        P("visit", "patch", None, None),
        P("visit", "patch"),
        P("visit", "patch"),
        P("visit", "patch"),
        P("visit", None, None),
        P(None, "patch"),
        P(None, "patch"),
    )
    return jax.shard_map(
        body, mesh=mesh, in_specs=placed, out_specs=P("visit", "patch", None, None), check_vma=False
    )
```

```python
import jax
import jax.numpy as jnp
import ml_dtypes
import numpy as np
from jax import lax
from jax.experimental import pallas as pl
from jax.experimental.pallas import tpu as pltpu
from jax.sharding import PartitionSpec as P

TILE = 128
KHALF = 15
HALO = 16
SPAN = TILE + 2 * HALO
SIGMAS = (1.5, 3.0, 5.0, 7.0)
DEGREES = (4, 2, 1, 0)
NPROF = 11
NBASIS = 25
NPOLY = 6
PT = 16
SKY = 2048
VIS = 2
GROUP = 3 * VIS * TILE
CH = 32
CHUNKS = TILE // CH
MAIN = NPROF * TILE
DEEP = MAIN + 3 * TILE
OWNERS = 16
VISITORS = 8
CAP = 4
MESH = pl.DeviceIdType.MESH


def profile_table():
    u = np.arange(-KHALF, KHALF + 1, dtype=np.float32)
    rows = []
    for sigma, degree in zip(SIGMAS, DEGREES):
        scaled = u / np.float32(sigma)
        envelope = np.exp(np.float32(-0.5) * scaled * scaled)
        for power in range(degree + 1):
            shaped = envelope * scaled**power
            rows.append(shaped / np.sum(np.abs(shaped)))
    return np.stack(rows).astype(np.float32)


def band_constants():
    profiles = profile_table()
    target = np.arange(TILE)

    def band(source):
        taps = source[:, None] - target[None, :] + KHALF
        inside = (taps >= 0) & (taps <= 2 * KHALF)
        return np.where(inside[None], profiles[:, np.clip(taps, 0, 2 * KHALF)], 0.0)

    columns = np.concatenate(
        [np.arange(TILE), np.arange(-HALO, 0), np.arange(TILE, TILE + HALO)]
    )
    across = band(columns).astype(ml_dtypes.bfloat16)
    down = band(np.arange(-HALO, CH + HALO))[:, :, :CH].transpose(0, 2, 1)
    down = down.reshape(NPROF * CH, CH + 2 * HALO).astype(ml_dtypes.bfloat16)
    return across, down


def basis_order():
    order, start = [], 0
    for degree in DEGREES:
        for j in range(degree + 1):
            order.append((start + j, [start + i for i in range(degree - j + 1)]))
        start += degree + 1
    return order


def build_weights(strip, kw_ref, across_ref, w_ref):
    lane = lax.broadcasted_iota(jnp.int32, (1, TILE), 1) + strip * TILE
    x = (lane.astype(jnp.float32) + 0.5) / SKY * 2.0 - 1.0
    xx = x * x
    unused = MAIN + NPROF * 2 * HALO
    w_ref[unused:, :] = jnp.zeros((DEEP - unused, GROUP), jnp.bfloat16)
    k = 0
    for j, sources in basis_order():
        for v in range(VIS):
            sums = [None, None, None]
            for n, source in enumerate(sources):
                c = [kw_ref[v, m, k + n] for m in range(NPOLY)]
                rows = (c[0] + c[1] * x + c[3] * xx, c[2] + c[4] * x, c[5])
                image = across_ref[source].astype(jnp.float32)
                for b in range(3):
                    term = rows[b] * image
                    sums[b] = term if sums[b] is None else sums[b] + term
            for b in range(3):
                at = (b * VIS + v) * TILE
                value = sums[b].astype(jnp.bfloat16)
                halo = MAIN + j * 2 * HALO
                w_ref[j * TILE : (j + 1) * TILE, at : at + TILE] = value[:TILE]
                w_ref[halo : halo + 2 * HALO, at : at + TILE] = value[TILE:]
        k += len(sources)


def match_chunk(part, padded_ref, down_ref, w_ref, columns_ref, matched_ref):
    @pl.loop(0, PT, unroll=True)
    def _(tile):
        top = pl.multiple_of(tile * TILE + part * CH, 16)
        rows = pl.ds(pl.multiple_of(tile * CH, 16), CH)
        both = jnp.dot(
            down_ref[...],
            padded_ref[pl.ds(top, CH + 2 * HALO), :],
            preferred_element_type=jnp.float32,
        )
        for group in range(3):
            total = None
            for q in range(min(4, NPROF - 4 * group)):
                j = 4 * group + q
                piece = both[j * CH : (j + 1) * CH]
                columns_ref[rows, j * TILE : (j + 1) * TILE] = piece[:, :TILE].astype(jnp.bfloat16)
                side = piece[:, TILE:]
                side = pltpu.roll(side, 2 * HALO * q, 1) if q else side
                total = side if total is None else total + side
            at = MAIN + group * TILE
            columns_ref[rows, at : at + TILE] = total.astype(jnp.bfloat16)

    half = VIS * TILE
    line = lax.broadcasted_iota(jnp.int32, (PT * CH, 1), 0)
    y = (line // CH * TILE + part * CH + line % CH).astype(jnp.float32)
    y = (y + 0.5) / SKY * 2.0 - 1.0
    total = jnp.zeros((PT * CH, half), jnp.float32)
    for power, factor in enumerate((None, y, y * y)):
        term = jnp.dot(
            columns_ref[...],
            w_ref[:, power * half : (power + 1) * half],
            preferred_element_type=jnp.float32,
        )
        total = total + (term if factor is None else factor * term)
    total = total.astype(jnp.bfloat16)
    for v in range(VIS):
        for tile in range(PT):
            matched_ref[v * PT + tile] = total[
                tile * CH : (tile + 1) * CH, v * TILE : (v + 1) * TILE
            ]


def remote(src, dst, send, recv, visit, patch):
    return pltpu.make_async_remote_copy(
        src_ref=src,
        dst_ref=dst,
        send_sem=send,
        recv_sem=recv,
        device_id={"visit": visit, "patch": patch},
        device_id_type=MESH,
    )


def kernel(
    source_ref, position_ref, flag_ref, kw_ref, science_ref, label_ref, weight_ref,
    prior_ref, prior_weight_ref, across_ref, down_ref, out_ref,
    w_ref, columns_ref, padded_ref, matched_ref, outgoing_ref, arrived_ref,
    back_0, back_1, back_2, back_3,
    acc_ref, pair_ref, ring_ref, side_ref, sum_ref, sum_pair_ref, sum_ring_ref,
    prior_vmem, labels_vmem, weights_vmem, labels_ref, weights_ref, coef_ref,
    local_sem, label_send, label_recv, weight_send, weight_recv, tile_send, tile_recv,
    pair_send, pair_recv, ring_send, ring_recv, side_send, side_recv, strip_send, strip_recv,
    sum_send, sum_recv, back_send, back_recv,
):
    visit = lax.axis_index("visit")
    me = lax.axis_index("patch")
    z, core = visit // 2, visit % 2
    twin = z * 2 + 1 - core
    returned = (back_0, back_1, back_2, back_3)
    own = core * 4 + z

    def peer(k):
        return lax.rem(me + k, OWNERS)

    def origin(k):
        return lax.rem(me + OWNERS - k, OWNERS)

    def other(k):
        return lax.rem(visit + k, VISITORS)

    def earlier(k):
        to = lax.rem(visit + VISITORS - k, VISITORS)
        return (to % 2) * 4 + to // 2

    prior_copies = [
        pltpu.make_async_copy(
            ref.at[pl.ds(pl.multiple_of(own * 256, 256), 256), :],
            prior_vmem.at[n],
            local_sem.at[n],
        )
        for n, ref in enumerate((prior_ref, prior_weight_ref))
    ]
    for copy in prior_copies:
        copy.start()

    barrier = pltpu.get_barrier_semaphore()

    @pl.loop(1, OWNERS)
    def _(k):
        pl.semaphore_signal(
            barrier, inc=1, device_id={"visit": visit, "patch": peer(k)}, device_id_type=MESH
        )

    @pl.loop(1, VISITORS)
    def _(k):
        pl.semaphore_signal(
            barrier, inc=1, device_id={"visit": other(k), "patch": me}, device_id_type=MESH
        )

    pl.semaphore_wait(barrier, OWNERS + VISITORS - 2)

    def label_copies(k, to, slot):
        return (
            remote(
                label_ref.at[to], labels_vmem.at[slot], label_send.at[k], label_recv.at[slot],
                visit, to,
            ),
            remote(
                weight_ref.at[to], weights_vmem.at[slot], weight_send.at[k], weight_recv.at[slot],
                visit, to,
            ),
        )

    def tile_copy(part, k, to, slot):
        return remote(
            outgoing_ref.at[part, to], arrived_ref.at[part, slot],
            tile_send.at[part, k], tile_recv.at[part, slot], visit, to,
        )

    def back_copy(part, k, to, slot):
        return remote(
            outgoing_ref.at[part, to], returned[part].at[slot],
            back_send.at[part, k], back_recv.at[part, slot], visit, to,
        )

    @pl.loop(1, OWNERS)
    def _(k):
        for copy in label_copies(k, peer(k), me):
            copy.start()

    def pack(part, to, target, at):
        rows = pl.ds(pl.multiple_of(part * CH, 16), CH)
        for c in range(CAP):
            target[part, at, c] = science_ref[source_ref[to * CAP + c], rows, :]

    @pl.loop(0, CHUNKS)
    def _(part):
        @pl.loop(1, OWNERS)
        def _(k):
            pack(part, peer(k), outgoing_ref, peer(k))
            tile_copy(part, k, peer(k), me).start()

        pack(part, me, arrived_ref, me)

    labels_vmem[me] = label_ref[me]
    weights_vmem[me] = weight_ref[me]

    @pl.loop(1, OWNERS)
    def _(k):
        for copy in label_copies(k, origin(k), origin(k)):
            copy.wait_recv()

    scalars = [
        pltpu.make_async_copy(labels_vmem, labels_ref, local_sem.at[2]),
        pltpu.make_async_copy(weights_vmem, weights_ref, local_sem.at[3]),
    ]
    for copy in scalars:
        copy.start()
    acc_ref[...] = jnp.zeros_like(acc_ref)
    sum_ref[...] = jnp.zeros_like(sum_ref)
    blank = jnp.zeros((HALO, 2 * TILE), jnp.bfloat16)
    padded_ref[:HALO, :] = blank
    padded_ref[HALO + SKY :, :] = blank
    for copy in scalars:
        copy.wait()

    @pl.loop(0, OWNERS)
    def _(at):
        for t in range(PT):
            total = 0.0
            for c in range(CAP):
                value = jnp.where(labels_ref[at, 0, c] % PT == t, weights_ref[at, 0, c], 0.0)
                coef_ref[(at * PT + t) * CAP + c] = value
                total = total + value
            sum_ref[t] += jnp.full((8, TILE), total, jnp.float32)

    sum_copy = remote(
        sum_ref.at[pl.ds((1 - core) * 8, 8)], sum_pair_ref, sum_send.at[0], sum_recv.at[0], twin, me
    )

    def sum_ring(k):
        to = lax.rem(z + k, 4)
        return remote(
            sum_ref.at[pl.ds(core * 8 + to * 2, 2)], sum_ring_ref.at[k - 1],
            sum_send.at[k], sum_recv.at[k], to * 2 + core, me,
        )

    sum_copy.start()
    build_weights(me, kw_ref, across_ref, w_ref)
    sum_copy.wait_recv()
    for n in range(8):
        sum_ref[core * 8 + n] += sum_pair_ref[n]
    for k in (1, 2, 3):
        sum_ring(k).start()
    for copy in prior_copies:
        copy.wait()

    def pair_copy(part):
        return remote(
            acc_ref.at[part, pl.ds((1 - core) * 8, 8)], pair_ref.at[part],
            pair_send.at[part], pair_recv.at[part], twin, me,
        )

    def ring_copy(part, k):
        to = lax.rem(z + k, 4)
        return remote(
            acc_ref.at[part, pl.ds(core * 8 + to * 2, 2)], ring_ref.at[part, k - 1],
            ring_send.at[part, k], ring_recv.at[part, k], to * 2 + core, me,
        )

    def lines(part, owner, n):
        return pl.multiple_of(HALO + owner * 256 + n * TILE + part * CH, 16)

    def side_copy(part, n, side):
        to = peer(1) if side == 0 else origin(1)
        return remote(
            padded_ref.at[pl.ds(lines(part, own, n), CH), pl.ds(0, TILE)],
            side_ref.at[part, side, n],
            side_send.at[part, side, n], side_recv.at[part, side, n], visit, to,
        )

    def strip_copy(part, n, k, owner):
        rows = padded_ref.at[pl.ds(lines(part, owner, n), CH), :]
        return remote(
            rows, rows, strip_send.at[part, n, k], strip_recv.at[part, n, k], other(k), me
        )

    def gather(part):
        @pl.loop(0, OWNERS)
        def _(k):
            at = origin(k)

            @pl.when(k > 0)
            def _():
                tile_copy(part, k, at, at).wait_recv()

            slots = [arrived_ref[part, at, c].astype(jnp.float32) for c in range(CAP)]
            for t in range(PT):
                value = acc_ref[part, t]
                for c in range(CAP):
                    value = value + coef_ref[(at * PT + t) * CAP + c] * slots[c]
                acc_ref[part, t] = value

        pair_copy(part).start()

    def reduce_pair(part):
        pair_copy(part).wait_recv()
        for k in (1, 2, 3, 0):
            to = lax.rem(z + k, 4)
            for n in range(2):
                acc_ref[part, core * 8 + to * 2 + n] += pair_ref[part, to * 2 + n]
            if k > 0:
                ring_copy(part, k).start()

    def finish_template(part):
        for k in (1, 2, 3):
            ring_copy(part, k).wait_recv()
        for n in range(2):
            total = acc_ref[part, own * 2 + n]
            weight_sum = sum_ref[own * 2 + n]
            for k in range(3):
                total = total + ring_ref[part, k, n]
                weight_sum = weight_sum + sum_ring_ref[k, n]
            rows = pl.ds(pl.multiple_of(n * TILE + part * CH, 16), CH)
            weight = prior_vmem[1, rows, :]
            template = (weight * prior_vmem[0, rows, :] + total) / (weight + weight_sum[:1])
            padded_ref[pl.ds(lines(part, own, n), CH), :TILE] = template.astype(jnp.bfloat16)
        for n in range(2):
            for side in range(2):
                side_copy(part, n, side).start()

    def spread_strip(part):
        lane = lax.broadcasted_iota(jnp.int32, (CH, TILE), 1)
        for n in range(2):
            for side in range(2):
                side_copy(part, n, side).wait_recv()
            left = pltpu.roll(side_ref[part, 0, n].astype(jnp.float32), HALO, 1)
            right = pltpu.roll(side_ref[part, 1, n].astype(jnp.float32), HALO, 1)
            halo = jnp.where(
                (lane < HALO) & (me > 0),
                left,
                jnp.where(
                    (lane >= HALO) & (lane < 2 * HALO) & (me < OWNERS - 1), right, 0.0
                ),
            )
            padded_ref[pl.ds(lines(part, own, n), CH), TILE:] = halo.astype(jnp.bfloat16)

            @pl.loop(1, VISITORS)
            def _(k):
                strip_copy(part, n, k, own).start()

    def wait_strips(part):
        @pl.loop(1, VISITORS)
        def _(k):
            for n in range(2):
                strip_copy(part, n, k, earlier(k)).wait_recv()

    @pl.loop(0, CHUNKS + 3)
    def _(step):
        @pl.when(step < CHUNKS)
        def _():
            gather(step)

        @pl.when((step >= 1) & (step < CHUNKS + 1))
        def _():
            reduce_pair(step - 1)

        @pl.when(step == 2)
        def _():
            for k in (1, 2, 3):
                sum_ring(k).wait_recv()

        @pl.when((step >= 2) & (step < CHUNKS + 2))
        def _():
            finish_template(step - 2)

        @pl.when(step >= 3)
        def _():
            spread_strip(step - 3)

    @pl.loop(0, CHUNKS)
    def _(part):
        @pl.loop(1, OWNERS)
        def _(k):
            tile_copy(part, k, peer(k), me).wait_send()

    @pl.loop(0, CHUNKS)
    def _(step):
        part = lax.rem(step + 1, CHUNKS)

        @pl.when(step == 0)
        def _():
            for early in range(CHUNKS - 1):
                wait_strips(early)

        @pl.when(step == 1)
        def _():
            wait_strips(CHUNKS - 1)

        match_chunk(part, padded_ref, down_ref, w_ref, columns_ref, matched_ref)

        @pl.loop(1, OWNERS)
        def _(k):
            to = peer(k)
            for c in range(CAP):
                outgoing_ref[part, to, c] = matched_ref[labels_ref[to, 0, c]]
            for q in range(CHUNKS):

                @pl.when(part == q)
                def _():
                    back_copy(q, k, to, me).start()

        for q in range(CHUNKS):

            @pl.when(part == q)
            def _():
                for c in range(CAP):
                    returned[q][me, c] = matched_ref[labels_ref[me, 0, c]]

    for step in range(CHUNKS):
        part = (step + 1) % CHUNKS
        rows = pl.ds(part * CH, CH)

        @pl.loop(1, OWNERS)
        def _(k):
            back_copy(part, k, origin(k), origin(k)).wait_recv()

        @pl.loop(0, VIS * PT)
        def _(n):
            at = position_ref[n]
            matched = returned[part][at // CAP, at % CAP].astype(jnp.float32)
            value = science_ref[n, rows, :].astype(jnp.float32) - matched
            out_ref[n, rows, :] = (value * flag_ref[n]).astype(jnp.bfloat16)

    sum_copy.wait_send()
    for k in (1, 2, 3):
        sum_ring(k).wait_send()

    @pl.loop(0, CHUNKS)
    def _(part):
        pair_copy(part).wait_send()
        for k in (1, 2, 3):
            ring_copy(part, k).wait_send()
        for n in range(2):
            for side in range(2):
                side_copy(part, n, side).wait_send()

            @pl.loop(1, VISITORS)
            def _(k):
                strip_copy(part, n, k, own).wait_send()

    for part in range(CHUNKS):

        @pl.loop(1, OWNERS)
        def _(k):
            back_copy(part, k, peer(k), me).wait_send()

    @pl.loop(1, OWNERS)
    def _(k):
        for copy in label_copies(k, peer(k), me):
            copy.wait_send()


def body(science, tile_ids, valid, weights, kernel_weight_terms, prior_template, prior_weight):
    slots = tile_ids.size
    length = OWNERS * CAP
    ids = tile_ids.reshape(slots)
    flag = valid.reshape(slots).astype(jnp.float32)
    destination = ids // PT
    order = jnp.arange(slots, dtype=jnp.int32)
    label = (order // tile_ids.shape[1]) * PT + ids % PT
    same = (destination[:, None] == destination[None, :]) & (order[:, None] > order[None, :])
    position = destination * CAP + jnp.sum(same.astype(jnp.int32), axis=1)
    placed = position[None, :] == jnp.arange(length, dtype=jnp.int32)[:, None]
    source = jnp.sum(jnp.where(placed, order[None, :], 0), axis=1)
    weighted = weights.reshape(slots).astype(jnp.float32) * flag
    spread = ((0, 0), (0, 0), (0, TILE - CAP))
    labels = jnp.sum(jnp.where(placed, label[None, :], 0), axis=1).reshape(OWNERS, 1, CAP)
    weight = jnp.sum(jnp.where(placed, weighted[None, :], 0.0), axis=1).reshape(OWNERS, 1, CAP)
    across, down = band_constants()
    vmem = pl.BlockSpec(memory_space=pltpu.VMEM)
    smem = pl.BlockSpec(memory_space=pltpu.SMEM)
    hbm = pl.BlockSpec(memory_space=pl.ANY)
    dma = pltpu.SemaphoreType.DMA
    result = pl.pallas_call(
        kernel,
        out_shape=jax.ShapeDtypeStruct((slots, TILE, TILE), jnp.bfloat16),
        in_specs=[smem, smem, smem, smem, vmem, vmem, vmem, hbm, hbm, vmem, vmem],
        out_specs=vmem,
        scratch_shapes=[
            pltpu.VMEM((DEEP, GROUP), jnp.bfloat16),
            pltpu.VMEM((PT * CH, DEEP), jnp.bfloat16),
            pltpu.VMEM((SKY + 2 * HALO, 2 * TILE), jnp.bfloat16),
            pltpu.VMEM((VIS * PT, CH, TILE), jnp.bfloat16),
            pltpu.VMEM((CHUNKS, OWNERS, CAP, CH, TILE), jnp.bfloat16),
            pltpu.VMEM((CHUNKS, OWNERS, CAP, CH, TILE), jnp.bfloat16),
            pltpu.VMEM((OWNERS, CAP, CH, TILE), jnp.bfloat16),
            pltpu.VMEM((OWNERS, CAP, CH, TILE), jnp.bfloat16),
            pltpu.VMEM((OWNERS, CAP, CH, TILE), jnp.bfloat16),
            pltpu.VMEM((OWNERS, CAP, CH, TILE), jnp.bfloat16),
            pltpu.VMEM((CHUNKS, PT, CH, TILE), jnp.float32),
            pltpu.VMEM((CHUNKS, PT // 2, CH, TILE), jnp.float32),
            pltpu.VMEM((CHUNKS, 3, 2, CH, TILE), jnp.float32),
            pltpu.VMEM((CHUNKS, 2, 2, CH, TILE), jnp.bfloat16),
            pltpu.VMEM((PT, 8, TILE), jnp.float32),
            pltpu.VMEM((PT // 2, 8, TILE), jnp.float32),
            pltpu.VMEM((3, 2, 8, TILE), jnp.float32),
            pltpu.VMEM((2, 2 * TILE, TILE), jnp.float32),
            pltpu.VMEM((OWNERS, 1, TILE), jnp.int32),
            pltpu.VMEM((OWNERS, 1, TILE), jnp.float32),
            pltpu.SMEM((OWNERS, 1, TILE), jnp.int32),
            pltpu.SMEM((OWNERS, 1, TILE), jnp.float32),
            pltpu.SMEM((OWNERS * PT * CAP,), jnp.float32),
            dma((4,)),
            dma((OWNERS,)),
            dma((OWNERS,)),
            dma((OWNERS,)),
            dma((OWNERS,)),
            dma((CHUNKS, OWNERS)),
            dma((CHUNKS, OWNERS)),
            dma((CHUNKS,)),
            dma((CHUNKS,)),
            dma((CHUNKS, 4)),
            dma((CHUNKS, 4)),
            dma((CHUNKS, 2, 2)),
            dma((CHUNKS, 2, 2)),
            dma((CHUNKS, 2, VISITORS)),
            dma((CHUNKS, 2, VISITORS)),
            dma((4,)),
            dma((4,)),
            dma((CHUNKS, OWNERS)),
            dma((CHUNKS, OWNERS)),
        ],
        compiler_params=pltpu.CompilerParams(
            vmem_limit_bytes=56 << 20, collective_id=0, has_side_effects=True
        ),
    )(
        source,
        position,
        flag,
        kernel_weight_terms.astype(jnp.float32),
        science.reshape(slots, TILE, TILE),
        jnp.pad(labels, spread),
        jnp.pad(weight, spread),
        prior_template,
        prior_weight,
        jnp.asarray(across),
        jnp.asarray(down),
    )
    return result.reshape(science.shape)


def solution(mesh):
    placed = (
        P("visit", "patch", None, None),
        P("visit", "patch"),
        P("visit", "patch"),
        P("visit", "patch"),
        P("visit", None, None),
        P(None, "patch"),
        P(None, "patch"),
    )
    return jax.shard_map(
        body, mesh=mesh, in_specs=placed, out_specs=P("visit", "patch", None, None), check_vma=False
    )
```

```python
import jax
import jax.numpy as jnp
import ml_dtypes
import numpy as np
from jax import lax
from jax.experimental import pallas as pl
from jax.experimental.pallas import tpu as pltpu
from jax.sharding import PartitionSpec as P

TILE = 128
KHALF = 15
HALO = 16
SPAN = TILE + 2 * HALO
SIGMAS = (1.5, 3.0, 5.0, 7.0)
DEGREES = (4, 2, 1, 0)
NPROF = 11
NBASIS = 25
NPOLY = 6
PT = 16
SKY = 2048
VIS = 2
GROUP = 3 * VIS * TILE
CH = 32
CHUNKS = TILE // CH
MAIN = NPROF * TILE
DEEP = MAIN + 3 * TILE
OWNERS = 16
VISITORS = 8
CAP = 4
MESH = pl.DeviceIdType.MESH


def profile_table():
    u = np.arange(-KHALF, KHALF + 1, dtype=np.float32)
    rows = []
    for sigma, degree in zip(SIGMAS, DEGREES):
        scaled = u / np.float32(sigma)
        envelope = np.exp(np.float32(-0.5) * scaled * scaled)
        for power in range(degree + 1):
            shaped = envelope * scaled**power
            rows.append(shaped / np.sum(np.abs(shaped)))
    return np.stack(rows).astype(np.float32)


def band_constants():
    profiles = profile_table()
    target = np.arange(TILE)

    def band(source):
        taps = source[:, None] - target[None, :] + KHALF
        inside = (taps >= 0) & (taps <= 2 * KHALF)
        return np.where(inside[None], profiles[:, np.clip(taps, 0, 2 * KHALF)], 0.0)

    columns = np.concatenate(
        [np.arange(TILE), np.arange(-HALO, 0), np.arange(TILE, TILE + HALO)]
    )
    across = band(columns).astype(ml_dtypes.bfloat16)
    down = band(np.arange(-HALO, CH + HALO))[:, :, :CH].transpose(0, 2, 1)
    down = down.reshape(NPROF * CH, CH + 2 * HALO).astype(ml_dtypes.bfloat16)
    return across, down


def basis_order():
    order, start = [], 0
    for degree in DEGREES:
        for j in range(degree + 1):
            order.append((start + j, [start + i for i in range(degree - j + 1)]))
        start += degree + 1
    return order


def build_weights(strip, kw_ref, across_ref, w_ref):
    lane = lax.broadcasted_iota(jnp.int32, (1, TILE), 1) + strip * TILE
    x = (lane.astype(jnp.float32) + 0.5) / SKY * 2.0 - 1.0
    xx = x * x
    unused = MAIN + NPROF * 2 * HALO
    w_ref[unused:, :] = jnp.zeros((DEEP - unused, GROUP), jnp.bfloat16)
    k = 0
    for j, sources in basis_order():
        for v in range(VIS):
            sums = [None, None, None]
            for n, source in enumerate(sources):
                c = [kw_ref[v, m, k + n] for m in range(NPOLY)]
                rows = (c[0] + c[1] * x + c[3] * xx, c[2] + c[4] * x, c[5])
                image = across_ref[source].astype(jnp.float32)
                for b in range(3):
                    term = rows[b] * image
                    sums[b] = term if sums[b] is None else sums[b] + term
            for b in range(3):
                at = (b * VIS + v) * TILE
                value = sums[b].astype(jnp.bfloat16)
                halo = MAIN + j * 2 * HALO
                w_ref[j * TILE : (j + 1) * TILE, at : at + TILE] = value[:TILE]
                w_ref[halo : halo + 2 * HALO, at : at + TILE] = value[TILE:]
        k += len(sources)


def match_chunk(part, padded_ref, down_ref, w_ref, columns_ref, matched_ref):
    first = (part == 0).astype(jnp.int32)
    last = (part == CHUNKS - 1).astype(jnp.int32)
    before = lax.rem(part + CHUNKS - 1, CHUNKS)
    after = lax.rem(part + 1, CHUNKS)

    @pl.loop(0, PT, unroll=True)
    def _(tile):
        rows = pl.ds(pl.multiple_of(tile * CH, 16), CH)
        window = jnp.concatenate(
            [
                padded_ref[before, tile + 1 - first, CH - HALO :, :],
                padded_ref[part, tile + 1],
                padded_ref[after, tile + 1 + last, :HALO, :],
            ],
            axis=0,
        )
        both = jnp.dot(down_ref[...], window, preferred_element_type=jnp.float32)
        for group in range(3):
            total = None
            for q in range(min(4, NPROF - 4 * group)):
                j = 4 * group + q
                piece = both[j * CH : (j + 1) * CH]
                columns_ref[rows, j * TILE : (j + 1) * TILE] = piece[:, :TILE].astype(jnp.bfloat16)
                side = piece[:, TILE:]
                side = pltpu.roll(side, 2 * HALO * q, 1) if q else side
                total = side if total is None else total + side
            at = MAIN + group * TILE
            columns_ref[rows, at : at + TILE] = total.astype(jnp.bfloat16)

    half = VIS * TILE
    line = lax.broadcasted_iota(jnp.int32, (PT * CH, 1), 0)
    y = (line // CH * TILE + part * CH + line % CH).astype(jnp.float32)
    y = (y + 0.5) / SKY * 2.0 - 1.0
    total = jnp.zeros((PT * CH, half), jnp.float32)
    for power, factor in enumerate((None, y, y * y)):
        term = jnp.dot(
            columns_ref[...],
            w_ref[:, power * half : (power + 1) * half],
            preferred_element_type=jnp.float32,
        )
        total = total + (term if factor is None else factor * term)
    total = total.astype(jnp.bfloat16)
    for v in range(VIS):
        for tile in range(PT):
            matched_ref[v * PT + tile] = total[
                tile * CH : (tile + 1) * CH, v * TILE : (v + 1) * TILE
            ]


def remote(src, dst, send, recv, visit, patch):
    return pltpu.make_async_remote_copy(
        src_ref=src,
        dst_ref=dst,
        send_sem=send,
        recv_sem=recv,
        device_id={"visit": visit, "patch": patch},
        device_id_type=MESH,
    )


def kernel(
    ids_ref, valid_ref, weights_ref, terms_ref, science_ref,
    prior_ref, prior_weight_ref, across_ref, down_ref, out_ref,
    w_ref, columns_ref, padded_ref, matched_ref, outgoing_ref, arrived_ref,
    back_0, back_1, back_2, back_3,
    acc_ref, give_ref, share_ref, edge_out, edge_ref, prior_vmem,
    slot_weight_vmem, terms_vmem, source_vmem, label_out, labels_vmem, coef_out, coefs_vmem,
    sum_out, sums_vmem,
    slot_weight_ref, kw_ref, source_ref, position_ref, labels_ref, coef_ref,
    local_sem, label_send, label_recv, coef_send, coef_recv, tile_send, tile_recv,
    share_send, share_recv, strip_send, strip_recv, edge_send, edge_recv,
    sum_send, sum_recv, back_send, back_recv,
):
    visit = lax.axis_index("visit")
    me = lax.axis_index("patch")
    own = visit
    returned = (back_0, back_1, back_2, back_3)
    slots = VIS * PT

    def peer(k):
        return lax.rem(me + k, OWNERS)

    def origin(k):
        return lax.rem(me + OWNERS - k, OWNERS)

    def other(k):
        return lax.rem(visit + k, VISITORS)

    def earlier(k):
        return lax.rem(visit + VISITORS - k, VISITORS)

    def neighbour(side):
        return peer(1) if side == 0 else origin(1)

    barrier = pltpu.get_barrier_semaphore()

    def greet(to_visit, to_patch):
        pl.semaphore_signal(
            barrier, inc=1, device_id={"visit": to_visit, "patch": to_patch}, device_id_type=MESH
        )

    @pl.loop(1, OWNERS)
    def _(k):
        greet(visit, peer(k))

    @pl.loop(1, VISITORS)
    def _(k):
        greet(other(k), me)
        greet(other(k), peer(1))
        greet(other(k), origin(1))

    prior_copies = [
        pltpu.make_async_copy(
            ref.at[pl.ds(pl.multiple_of(own * 256, 256), 256), :],
            prior_vmem.at[n],
            local_sem.at[n],
        )
        for n, ref in enumerate((prior_ref, prior_weight_ref))
    ]
    for copy in prior_copies:
        copy.start()
    slot_weight_vmem[...] = weights_ref[...].astype(jnp.float32)
    terms_vmem[...] = terms_ref[...].astype(jnp.float32)
    weight_copy = pltpu.make_async_copy(slot_weight_vmem, slot_weight_ref, local_sem.at[2])
    terms_copy = pltpu.make_async_copy(terms_vmem, kw_ref, local_sem.at[3])
    weight_copy.start()
    terms_copy.start()

    @pl.loop(0, slots)
    def _(n):
        strip = ids_ref[n // PT, n % PT] // PT
        rank = 0
        for m in range(slots):
            same = (ids_ref[m // PT, m % PT] // PT == strip) & (m < n)
            rank = rank + same.astype(jnp.int32)
        position_ref[n] = strip * CAP + rank

    lane = lax.broadcasted_iota(jnp.int32, (1, TILE), 1)
    source = jnp.zeros((1, TILE), jnp.int32)
    label = jnp.zeros((1, TILE), jnp.int32)
    for n in range(slots):
        here = lane == position_ref[n]
        source = jnp.where(here, n, source)
        label = jnp.where(here, n // PT * PT + ids_ref[n // PT, n % PT] % PT, label)
    source_vmem[...] = source
    label_out[...] = label
    source_copy = pltpu.make_async_copy(source_vmem, source_ref, local_sem.at[4])
    source_copy.start()
    weight_copy.wait()
    owner_row = lax.broadcasted_iota(jnp.int32, (OWNERS, TILE), 0)
    entry = lax.broadcasted_iota(jnp.int32, (OWNERS, TILE), 1)
    coefs = jnp.zeros((OWNERS, TILE), jnp.float32)
    for n in range(slots):
        v, s = n // PT, n % PT
        at = position_ref[n]
        here = (owner_row == at // CAP) & (entry == ids_ref[v, s] % PT * CAP + at % CAP)
        weight = slot_weight_ref[v, s] * valid_ref[v, s].astype(jnp.float32)
        coefs = jnp.where(here, weight, coefs)
    for to in range(OWNERS):
        coef_out[to] = coefs[to : to + 1]
    source_copy.wait()
    terms_copy.wait()

    pl.semaphore_wait(barrier, OWNERS - 1 + 3 * (VISITORS - 1))

    def coef_copy(k, to, slot):
        return remote(
            coef_out.at[to], coefs_vmem.at[slot], coef_send.at[k], coef_recv.at[slot], visit, to
        )

    def label_copy(k, to, slot):
        return remote(
            label_out, labels_vmem.at[slot], label_send.at[k], label_recv.at[slot], visit, to
        )

    def tile_copy(part, k, to, slot):
        return remote(
            outgoing_ref.at[part, to], arrived_ref.at[part, slot],
            tile_send.at[part, k], tile_recv.at[part, slot], visit, to,
        )

    def back_copy(part, k, to, slot):
        return remote(
            outgoing_ref.at[part, to], returned[part].at[slot],
            back_send.at[part, k], back_recv.at[part, slot], visit, to,
        )

    def sum_copy(k):
        return remote(sum_out, sums_vmem.at[k], sum_send.at[k], sum_recv.at[k], other(k), me)

    def share_copy(part, k):
        return remote(
            give_ref.at[part, other(k)], share_ref.at[part, k],
            share_send.at[part, k], share_recv.at[part, k], other(k), me,
        )

    def strip_copy(part, k, owner):
        rows = padded_ref.at[part, pl.ds(1 + 2 * owner, 2), :, pl.ds(0, TILE)]
        return remote(rows, rows, strip_send.at[part, k], strip_recv.at[part, k], other(k), me)

    def edge_copy(part, side, k):
        return remote(
            edge_out.at[part], edge_ref.at[part, side, k],
            edge_send.at[part, side, k], edge_recv.at[part, side, k], other(k), neighbour(side),
        )

    def pack(part, to, target, at):
        rows = pl.ds(pl.multiple_of(part * CH, 16), CH)
        for c in range(CAP):
            target[part, at, c] = science_ref[source_ref[0, to * CAP + c], rows, :]

    @pl.loop(1, OWNERS)
    def _(k):
        coef_copy(k, peer(k), me).start()

    @pl.loop(0, CHUNKS)
    def _(part):
        @pl.loop(1, OWNERS)
        def _(k):
            pack(part, peer(k), outgoing_ref, peer(k))
            tile_copy(part, k, peer(k), me).start()

        pack(part, me, arrived_ref, me)

    @pl.loop(1, OWNERS)
    def _(k):
        label_copy(k, peer(k), me).start()

    labels_vmem[me] = label_out[...]
    coefs_vmem[me] = coef_out[me]

    @pl.loop(1, OWNERS)
    def _(k):
        coef_copy(k, origin(k), origin(k)).wait_recv()

    coef_local = pltpu.make_async_copy(coefs_vmem, coef_ref, local_sem.at[5])
    coef_local.start()
    row = coefs_vmem[0]
    for at in range(1, OWNERS):
        row = row + coefs_vmem[at]
    sum_out[...] = row

    @pl.loop(1, VISITORS)
    def _(k):
        sum_copy(k).start()

    build_weights(me, kw_ref, across_ref, w_ref)
    blank = jnp.zeros((CH, 2 * TILE), jnp.bfloat16)
    for part in range(CHUNKS):
        padded_ref[part, 0] = blank
        padded_ref[part, PT + 1] = blank
    for copy in prior_copies:
        copy.wait()
    coef_local.wait()

    def add_slots(part, at, fresh):
        tiles = [arrived_ref[part, at, c].astype(jnp.float32) for c in range(CAP)]
        for t in range(PT):
            value = None if fresh else acc_ref[t]
            for c in range(CAP):
                term = coef_ref[at, 0, t * CAP + c] * tiles[c]
                value = term if value is None else value + term
            acc_ref[t] = value

    def gather(part):
        add_slots(part, me, True)

        @pl.loop(1, OWNERS)
        def _(k):
            at = origin(k)
            tile_copy(part, k, at, at).wait_recv()
            add_slots(part, at, False)

        for to in range(VISITORS):
            for n in range(2):
                give_ref[part, to, n] = acc_ref[2 * to + n].astype(jnp.bfloat16)

        @pl.loop(1, VISITORS)
        def _(k):
            share_copy(part, k).start()

    def finish(part):
        @pl.loop(1, VISITORS)
        def _(k):
            share_copy(part, k).wait_recv()

        total_row = sum_out[...]
        for k in range(1, VISITORS):
            total_row = total_row + sums_vmem[k]
        spot = lax.broadcasted_iota(jnp.int32, (HALO, TILE), 1)
        packed = jnp.zeros((HALO, TILE), jnp.float32)
        for n in range(2):
            total = acc_ref[own * 2 + n]
            for k in range(1, VISITORS):
                total = total + share_ref[part, k, n].astype(jnp.float32)
            weight_sum = jnp.sum(
                jnp.where(lane // CAP == own * 2 + n, total_row, 0.0), axis=1, keepdims=True
            )
            rows = pl.ds(pl.multiple_of(n * TILE + part * CH, 16), CH)
            weight = prior_vmem[1, rows, :]
            template = (weight * prior_vmem[0, rows, :] + total) / (weight + weight_sum)
            template = template.astype(jnp.bfloat16)
            padded_ref[part, 1 + own * 2 + n, :, :TILE] = template
            wide = template.astype(jnp.float32)
            for h in range(2):
                g = 2 * n + h
                moved = pltpu.roll(
                    wide[h * HALO : (h + 1) * HALO], (2 * HALO * g + HALO) % TILE, 1
                )
                packed = jnp.where(spot // (2 * HALO) == g, moved, packed)
        edge_out[part] = packed.astype(jnp.bfloat16)

        @pl.loop(0, VISITORS)
        def _(k):
            for side in range(2):
                edge_copy(part, side, k).start()

        @pl.loop(1, VISITORS)
        def _(k):
            strip_copy(part, k, own).start()

    def wait_strips(part):
        spot = lax.broadcasted_iota(jnp.int32, (HALO, TILE), 1)

        @pl.loop(1, VISITORS)
        def _(k):
            strip_copy(part, k, earlier(k)).wait_recv()

        @pl.loop(0, VISITORS)
        def _(k):
            for side in range(2):
                edge_copy(part, side, k).wait_recv()
            left = jnp.where(me > 0, edge_ref[part, 0, k].astype(jnp.float32), 0.0)
            right = jnp.where(me < OWNERS - 1, edge_ref[part, 1, k].astype(jnp.float32), 0.0)
            both = jnp.where(spot % (2 * HALO) < HALO, left, right)
            for g in range(4):
                moved = pltpu.roll(both, (TILE - 2 * HALO * g) % TILE, 1) if g else both
                moved = jnp.where(spot < 2 * HALO, moved, 0.0).astype(jnp.bfloat16)
                n, h = g // 2, g % 2
                padded_ref[
                    part, 1 + earlier(k) * 2 + n, h * HALO : (h + 1) * HALO, TILE:
                ] = moved

    @pl.loop(0, CHUNKS)
    def _(step):
        gather(step)

        @pl.when(step == 0)
        def _():
            @pl.loop(1, VISITORS)
            def _(k):
                sum_copy(k).wait_recv()

        @pl.when(step < CHUNKS - 1)
        def _():
            finish(step)

    @pl.loop(1, OWNERS)
    def _(k):
        label_copy(k, origin(k), origin(k)).wait_recv()

    label_local = pltpu.make_async_copy(labels_vmem, labels_ref, local_sem.at[6])
    label_local.start()

    @pl.loop(0, CHUNKS)
    def _(part):
        @pl.loop(1, OWNERS)
        def _(k):
            tile_copy(part, k, peer(k), me).wait_send()

    @pl.loop(0, CHUNKS - 1)
    def _(part):
        wait_strips(part)

    label_local.wait()

    @pl.loop(0, CHUNKS)
    def _(step):
        part = lax.rem(step + 1, CHUNKS)

        @pl.when(step == 1)
        def _():
            wait_strips(CHUNKS - 1)

        match_chunk(part, padded_ref, down_ref, w_ref, columns_ref, matched_ref)

        @pl.when(step == 0)
        def _():
            finish(CHUNKS - 1)

        @pl.loop(1, OWNERS)
        def _(k):
            to = peer(k)
            for c in range(CAP):
                outgoing_ref[part, to, c] = matched_ref[labels_ref[to, 0, me * CAP + c]]
            for q in range(CHUNKS):

                @pl.when(part == q)
                def _():
                    back_copy(q, k, to, me).start()

        for q in range(CHUNKS):

            @pl.when(part == q)
            def _():
                for c in range(CAP):
                    returned[q][me, c] = matched_ref[labels_ref[me, 0, me * CAP + c]]

    for step in range(CHUNKS):
        part = (step + 1) % CHUNKS
        rows = pl.ds(part * CH, CH)

        @pl.loop(1, OWNERS)
        def _(k):
            back_copy(part, k, origin(k), origin(k)).wait_recv()

        @pl.loop(0, slots)
        def _(n):
            at = position_ref[n]
            matched = returned[part][at // CAP, at % CAP].astype(jnp.float32)
            value = science_ref[n, rows, :].astype(jnp.float32) - matched
            keep = valid_ref[n // PT, n % PT].astype(jnp.float32)
            out_ref[n, rows, :] = (value * keep).astype(jnp.bfloat16)

    @pl.loop(1, OWNERS)
    def _(k):
        coef_copy(k, peer(k), me).wait_send()
        label_copy(k, peer(k), me).wait_send()

    @pl.loop(1, VISITORS)
    def _(k):
        sum_copy(k).wait_send()

    @pl.loop(0, CHUNKS)
    def _(part):
        @pl.loop(1, VISITORS)
        def _(k):
            share_copy(part, k).wait_send()
            strip_copy(part, k, own).wait_send()

        @pl.loop(0, VISITORS)
        def _(k):
            for side in range(2):
                edge_copy(part, side, k).wait_send()

    for part in range(CHUNKS):

        @pl.loop(1, OWNERS)
        def _(k):
            back_copy(part, k, peer(k), me).wait_send()


def body(science, tile_ids, valid, weights, kernel_weight_terms, prior_template, prior_weight):
    slots = tile_ids.size
    across, down = band_constants()
    vmem = pl.BlockSpec(memory_space=pltpu.VMEM)
    smem = pl.BlockSpec(memory_space=pltpu.SMEM)
    hbm = pl.BlockSpec(memory_space=pl.ANY)
    dma = pltpu.SemaphoreType.DMA
    f32, bf16, i32 = jnp.float32, jnp.bfloat16, jnp.int32
    result = pl.pallas_call(
        kernel,
        out_shape=jax.ShapeDtypeStruct((slots, TILE, TILE), jnp.bfloat16),
        in_specs=[smem, smem, vmem, vmem, vmem, hbm, hbm, vmem, vmem],
        out_specs=vmem,
        scratch_shapes=[
            pltpu.VMEM((DEEP, GROUP), bf16),
            pltpu.VMEM((PT * CH, DEEP), bf16),
            pltpu.VMEM((CHUNKS, PT + 2, CH, 2 * TILE), bf16),
            pltpu.VMEM((VIS * PT, CH, TILE), bf16),
            pltpu.VMEM((CHUNKS, OWNERS, CAP, CH, TILE), bf16),
            pltpu.VMEM((CHUNKS, OWNERS, CAP, CH, TILE), bf16),
            pltpu.VMEM((OWNERS, CAP, CH, TILE), bf16),
            pltpu.VMEM((OWNERS, CAP, CH, TILE), bf16),
            pltpu.VMEM((OWNERS, CAP, CH, TILE), bf16),
            pltpu.VMEM((OWNERS, CAP, CH, TILE), bf16),
            pltpu.VMEM((PT, CH, TILE), f32),
            pltpu.VMEM((CHUNKS, VISITORS, 2, CH, TILE), bf16),
            pltpu.VMEM((CHUNKS, VISITORS, 2, CH, TILE), bf16),
            pltpu.VMEM((CHUNKS, HALO, TILE), bf16),
            pltpu.VMEM((CHUNKS, 2, VISITORS, HALO, TILE), bf16),
            pltpu.VMEM((2, 2 * TILE, TILE), f32),
            pltpu.VMEM(weights.shape, f32),
            pltpu.VMEM(kernel_weight_terms.shape, f32),
            pltpu.VMEM((1, TILE), i32),
            pltpu.VMEM((1, TILE), i32),
            pltpu.VMEM((OWNERS, 1, TILE), i32),
            pltpu.VMEM((OWNERS, 1, TILE), f32),
            pltpu.VMEM((OWNERS, 1, TILE), f32),
            pltpu.VMEM((1, TILE), f32),
            pltpu.VMEM((VISITORS, 1, TILE), f32),
            pltpu.SMEM(weights.shape, f32),
            pltpu.SMEM(kernel_weight_terms.shape, f32),
            pltpu.SMEM((1, TILE), i32),
            pltpu.SMEM((slots,), i32),
            pltpu.SMEM((OWNERS, 1, TILE), i32),
            pltpu.SMEM((OWNERS, 1, TILE), f32),
            dma((7,)),
            dma((OWNERS,)),
            dma((OWNERS,)),
            dma((OWNERS,)),
            dma((OWNERS,)),
            dma((CHUNKS, OWNERS)),
            dma((CHUNKS, OWNERS)),
            dma((CHUNKS, VISITORS)),
            dma((CHUNKS, VISITORS)),
            dma((CHUNKS, VISITORS)),
            dma((CHUNKS, VISITORS)),
            dma((CHUNKS, 2, VISITORS)),
            dma((CHUNKS, 2, VISITORS)),
            dma((VISITORS,)),
            dma((VISITORS,)),
            dma((CHUNKS, OWNERS)),
            dma((CHUNKS, OWNERS)),
        ],
        compiler_params=pltpu.CompilerParams(
            vmem_limit_bytes=56 << 20, collective_id=0, has_side_effects=True
        ),
    )(
        tile_ids,
        valid,
        weights,
        kernel_weight_terms,
        science.reshape(slots, TILE, TILE),
        prior_template,
        prior_weight,
        jnp.asarray(across),
        jnp.asarray(down),
    )
    return result.reshape(science.shape)


def solution(mesh):
    placed = (
        P("visit", "patch", None, None),
        P("visit", "patch"),
        P("visit", "patch"),
        P("visit", "patch"),
        P("visit", None, None),
        P(None, "patch"),
        P(None, "patch"),
    )
    return jax.shard_map(
        body, mesh=mesh, in_specs=placed, out_specs=P("visit", "patch", None, None), check_vma=False
    )
```

```python
import jax
import jax.numpy as jnp
import ml_dtypes
import numpy as np
from jax import lax
from jax.experimental import pallas as pl
from jax.experimental.pallas import tpu as pltpu
from jax.sharding import PartitionSpec as P

TILE = 128
KHALF = 15
HALO = 16
SPAN = TILE + 2 * HALO
SIGMAS = (1.5, 3.0, 5.0, 7.0)
DEGREES = (4, 2, 1, 0)
NPROF = 11
NBASIS = 25
NPOLY = 6
PT = 16
SKY = 2048
VIS = 2
GROUP = 3 * VIS * TILE
CH = 32
CHUNKS = TILE // CH
GATHERED = 5
MAIN = NPROF * TILE
DEEP = MAIN + 3 * TILE
OWNERS = 16
VISITORS = 8
CAP = 4
MESH = pl.DeviceIdType.MESH


def profile_table():
    u = np.arange(-KHALF, KHALF + 1, dtype=np.float32)
    rows = []
    for sigma, degree in zip(SIGMAS, DEGREES):
        scaled = u / np.float32(sigma)
        envelope = np.exp(np.float32(-0.5) * scaled * scaled)
        for power in range(degree + 1):
            shaped = envelope * scaled**power
            rows.append(shaped / np.sum(np.abs(shaped)))
    return np.stack(rows).astype(np.float32)


def band_constants():
    profiles = profile_table()
    target = np.arange(TILE)

    def band(source):
        taps = source[:, None] - target[None, :] + KHALF
        inside = (taps >= 0) & (taps <= 2 * KHALF)
        return np.where(inside[None], profiles[:, np.clip(taps, 0, 2 * KHALF)], 0.0)

    columns = np.concatenate(
        [np.arange(TILE), np.arange(-HALO, 0), np.arange(TILE, TILE + HALO)]
    )
    across = band(columns).astype(ml_dtypes.bfloat16)
    down = band(np.arange(-HALO, CH + HALO))[:, :, :CH].transpose(0, 2, 1)
    down = down.reshape(NPROF * CH, CH + 2 * HALO).astype(ml_dtypes.bfloat16)
    return across, down


def basis_order():
    order, start = [], 0
    for degree in DEGREES:
        for j in range(degree + 1):
            order.append((start + j, [start + i for i in range(degree - j + 1)]))
        start += degree + 1
    return order


def build_weights(strip, kw_ref, across_ref, w_ref):
    lane = lax.broadcasted_iota(jnp.int32, (1, TILE), 1) + strip * TILE
    x = (lane.astype(jnp.float32) + 0.5) / SKY * 2.0 - 1.0
    xx = x * x
    unused = MAIN + NPROF * 2 * HALO
    w_ref[unused:, :] = jnp.zeros((DEEP - unused, GROUP), jnp.bfloat16)
    k = 0
    for j, sources in basis_order():
        for v in range(VIS):
            sums = [None, None, None]
            for n, source in enumerate(sources):
                c = [kw_ref[m, v, k + n] for m in range(NPOLY)]
                rows = (c[0] + c[1] * x + c[3] * xx, c[2] + c[4] * x, c[5])
                image = across_ref[source].astype(jnp.float32)
                for b in range(3):
                    term = rows[b] * image
                    sums[b] = term if sums[b] is None else sums[b] + term
            for b in range(3):
                at = (b * VIS + v) * TILE
                value = sums[b].astype(jnp.bfloat16)
                halo = MAIN + j * 2 * HALO
                w_ref[j * TILE : (j + 1) * TILE, at : at + TILE] = value[:TILE]
                w_ref[halo : halo + 2 * HALO, at : at + TILE] = value[TILE:]
        k += len(sources)


def match_chunk(part, padded_ref, down_ref, w_ref, columns_ref, matched_ref):
    first = (part == 0).astype(jnp.int32)
    last = (part == CHUNKS - 1).astype(jnp.int32)
    before = lax.rem(part + CHUNKS - 1, CHUNKS)
    after = lax.rem(part + 1, CHUNKS)

    @pl.loop(0, PT, unroll=True)
    def _(tile):
        rows = pl.ds(pl.multiple_of(tile * CH, 16), CH)
        window = jnp.concatenate(
            [
                padded_ref[before, tile + 1 - first, CH - HALO :, :],
                padded_ref[part, tile + 1],
                padded_ref[after, tile + 1 + last, :HALO, :],
            ],
            axis=0,
        )
        both = jnp.dot(down_ref[...], window, preferred_element_type=jnp.float32)
        for group in range(3):
            total = None
            for q in range(min(4, NPROF - 4 * group)):
                j = 4 * group + q
                piece = both[j * CH : (j + 1) * CH]
                columns_ref[rows, j * TILE : (j + 1) * TILE] = piece[:, :TILE].astype(jnp.bfloat16)
                side = piece[:, TILE:]
                side = pltpu.roll(side, 2 * HALO * q, 1) if q else side
                total = side if total is None else total + side
            at = MAIN + group * TILE
            columns_ref[rows, at : at + TILE] = total.astype(jnp.bfloat16)

    half = VIS * TILE
    line = lax.broadcasted_iota(jnp.int32, (PT * CH, 1), 0)
    y = ((line >> 5) * TILE + part * CH + (line & (CH - 1))).astype(jnp.float32)
    y = (y + 0.5) / SKY * 2.0 - 1.0
    total = jnp.zeros((PT * CH, half), jnp.float32)
    for power, factor in enumerate((None, y, y * y)):
        term = jnp.dot(
            columns_ref[...],
            w_ref[:, power * half : (power + 1) * half],
            preferred_element_type=jnp.float32,
        )
        total = total + (term if factor is None else factor * term)
    total = total.astype(jnp.bfloat16)
    for v in range(VIS):
        for tile in range(PT):
            matched_ref[v * PT + tile] = total[
                tile * CH : (tile + 1) * CH, v * TILE : (v + 1) * TILE
            ]


def remote(src, dst, send, recv, visit, patch):
    return pltpu.make_async_remote_copy(
        src_ref=src,
        dst_ref=dst,
        send_sem=send,
        recv_sem=recv,
        device_id={"visit": visit, "patch": patch},
        device_id_type=MESH,
    )


def kernel(
    ids_ref, valid_ref, weights_ref, terms_ref, science_hbm,
    prior_ref, prior_weight_ref, across_hbm, down_hbm, out_ref,
    out_vmem, science_ref, across_ref, down_ref,
    w_ref, columns_ref, padded_ref, matched_ref, outgoing_ref, arrived_ref,
    back_0, back_1, back_2, back_3,
    back_out, acc_ref, own_ref, give_ref, share_ref, edge_out, edge_ref, prior_vmem,
    slot_weight_vmem, terms_vmem, source_vmem, label_out, labels_vmem, coef_out, coefs_vmem,
    sum_out, sums_vmem,
    slot_weight_ref, kw_ref, source_ref, position_ref, labels_ref, coef_ref,
    local_sem, label_send, label_recv, coef_send, coef_recv, tile_send, tile_recv,
    share_send, share_recv, strip_send, strip_recv, edge_send, edge_recv,
    sum_send, sum_recv, back_send, back_recv,
):
    visit = lax.axis_index("visit")
    me = lax.axis_index("patch")
    own = visit
    returned = (back_0, back_1, back_2, back_3)
    slots = VIS * PT

    def peer(k):
        return lax.rem(me + k, OWNERS)

    def origin(k):
        return lax.rem(me + OWNERS - k, OWNERS)

    def other(k):
        return lax.rem(visit + k, VISITORS)

    def earlier(k):
        return lax.rem(visit + VISITORS - k, VISITORS)

    def neighbour(side):
        return peer(1) if side == 0 else origin(1)

    science_copy = pltpu.make_async_copy(science_hbm, science_ref, local_sem.at[7])
    across_copy = pltpu.make_async_copy(across_hbm, across_ref, local_sem.at[8])
    down_copy = pltpu.make_async_copy(down_hbm, down_ref, local_sem.at[9])
    science_copy.start()
    barrier = pltpu.get_barrier_semaphore()

    def greet(to_visit, to_patch):
        pl.semaphore_signal(
            barrier, inc=1, device_id={"visit": to_visit, "patch": to_patch}, device_id_type=MESH
        )

    @pl.loop(1, OWNERS)
    def _(k):
        greet(visit, peer(k))

    @pl.loop(1, VISITORS)
    def _(k):
        greet(other(k), me)
        greet(other(k), peer(1))
        greet(other(k), origin(1))

    prior_copies = [
        pltpu.make_async_copy(
            ref.at[pl.ds(pl.multiple_of(own * 256, 256), 256), :],
            prior_vmem.at[n],
            local_sem.at[n],
        )
        for n, ref in enumerate((prior_ref, prior_weight_ref))
    ]
    for copy in prior_copies:
        copy.start()
    across_copy.start()
    down_copy.start()
    slot_weight_vmem[...] = weights_ref[...].astype(jnp.float32)
    terms_vmem[...] = terms_ref[...].astype(jnp.float32)
    weight_copy = pltpu.make_async_copy(slot_weight_vmem, slot_weight_ref, local_sem.at[2])
    terms_copy = pltpu.make_async_copy(terms_vmem, kw_ref, local_sem.at[3])
    weight_copy.start()
    terms_copy.start()

    ids = [ids_ref[n // PT, n % PT] for n in range(slots)]
    strips = [value >> 4 for value in ids]
    tiles = [value & (PT - 1) for value in ids]
    for n in range(slots):
        rank = 0
        for m in range(n):
            rank = rank + jnp.where(strips[m] == strips[n], 1, 0)
        position_ref[n] = strips[n] * CAP + rank

    lane = lax.broadcasted_iota(jnp.int32, (1, TILE), 1)
    source = jnp.zeros((1, TILE), jnp.int32)
    label = jnp.zeros((1, TILE), jnp.int32)
    for n in range(slots):
        here = lane == position_ref[n]
        source = jnp.where(here, n, source)
        label = jnp.where(here, n // PT * PT + tiles[n], label)
    source_vmem[...] = source
    label_out[...] = label
    source_copy = pltpu.make_async_copy(source_vmem, source_ref, local_sem.at[4])
    source_copy.start()
    weight_copy.wait()
    owner_row = lax.broadcasted_iota(jnp.int32, (OWNERS, TILE), 0)
    entry = lax.broadcasted_iota(jnp.int32, (OWNERS, TILE), 1)
    coefs = jnp.zeros((OWNERS, TILE), jnp.float32)
    for n in range(slots):
        v, s = n // PT, n % PT
        at = position_ref[n]
        here = (owner_row == at >> 2) & (entry == tiles[n] * CAP + (at & (CAP - 1)))
        weight = slot_weight_ref[v, s] * valid_ref[v, s].astype(jnp.float32)
        coefs = jnp.where(here, weight, coefs)
    for to in range(OWNERS):
        coef_out[to] = coefs[to : to + 1]
    source_copy.wait()
    terms_copy.wait()
    science_copy.wait()

    pl.semaphore_wait(barrier, OWNERS - 1 + 3 * (VISITORS - 1))

    def coef_copy(k, to, slot):
        return remote(
            coef_out.at[to], coefs_vmem.at[slot], coef_send, coef_recv, visit, to
        )

    def label_copy(k, to, slot):
        return remote(
            label_out, labels_vmem.at[slot], label_send, label_recv, visit, to
        )

    def tile_copy(part, k, to, slot):
        return remote(
            outgoing_ref.at[part, to], arrived_ref.at[part, slot],
            tile_send, tile_recv.at[part, (k - 1) // GATHERED], visit, to,
        )

    def back_copy(part, k, to, slot):
        return remote(
            back_out.at[part, to], returned[part].at[slot],
            back_send, back_recv.at[part], visit, to,
        )

    def arrive(block, semaphore):
        remote(block, block, semaphore, semaphore, visit, peer(1)).wait_recv()

    def leave(block, semaphore):
        remote(block, block, semaphore, semaphore, visit, peer(1)).wait_send()

    def sum_copy(k):
        return remote(sum_out, sums_vmem.at[k], sum_send, sum_recv, other(k), me)

    def share_copy(part, k):
        return remote(
            give_ref.at[part, other(k)], share_ref.at[part, k],
            share_send, share_recv.at[part], other(k), me,
        )

    def strip_copy(part, k, owner):
        rows = padded_ref.at[part, pl.ds(1 + 2 * owner, 2), :, pl.ds(0, TILE)]
        return remote(rows, rows, strip_send, strip_recv.at[part], other(k), me)

    def edge_copy(part, side, k):
        return remote(
            edge_out.at[part], edge_ref.at[part, side, k],
            edge_send, edge_recv.at[part], other(k), neighbour(side),
        )

    def pack(part, to, target, at):
        rows = pl.ds(pl.multiple_of(part * CH, 16), CH)
        for c in range(CAP):
            target[part, at, c] = science_ref[source_ref[0, to * CAP + c], rows, :]

    @pl.loop(1, OWNERS)
    def _(k):
        coef_copy(k, peer(k), me).start()
        label_copy(k, peer(k), me).start()

    @pl.loop(0, CHUNKS)
    def _(part):
        @pl.loop(1, OWNERS)
        def _(k):
            pack(part, peer(k), outgoing_ref, peer(k))
            tile_copy(part, k, peer(k), me).start()

        pack(part, me, arrived_ref, me)

    labels_vmem[me] = label_out[...]
    coefs_vmem[me] = coef_out[me]

    arrive(coefs_vmem.at[pl.ds(0, OWNERS - 1)], coef_recv)

    coef_local = pltpu.make_async_copy(coefs_vmem, coef_ref, local_sem.at[5])
    coef_local.start()
    row = coefs_vmem[0]
    for at in range(1, OWNERS):
        row = row + coefs_vmem[at]
    sum_out[...] = row

    @pl.loop(1, VISITORS)
    def _(k):
        sum_copy(k).start()

    across_copy.wait()
    down_copy.wait()
    build_weights(me, kw_ref, across_ref, w_ref)
    blank = jnp.zeros((CH, 2 * TILE), jnp.bfloat16)
    for part in range(CHUNKS):
        padded_ref[part, 0] = blank
        padded_ref[part, PT + 1] = blank
    for copy in prior_copies:
        copy.wait()
    coef_local.wait()

    def add_slots(part, at, fresh):
        tiles = [arrived_ref[part, at, c].astype(jnp.float32) for c in range(CAP)]
        for t in range(PT):
            value = None if fresh else acc_ref[t]
            for c in range(CAP):
                term = coef_ref[at, 0, t * CAP + c] * tiles[c]
                value = term if value is None else value + term
            acc_ref[t] = value

    def gather(part):
        add_slots(part, me, True)

        @pl.loop(0, (OWNERS - 1) // GATHERED)
        def _(group):
            arrive(arrived_ref.at[part, pl.ds(0, GATHERED)], tile_recv.at[part, group])

            @pl.loop(1, GATHERED + 1)
            def _(k):
                add_slots(part, origin(group * GATHERED + k), False)

        for to in range(VISITORS):
            for n in range(2):
                give_ref[part, to, n] = acc_ref[2 * to + n].astype(jnp.bfloat16)

        @pl.loop(1, VISITORS)
        def _(k):
            share_copy(part, k).start()

        own_ref[part] = acc_ref[pl.ds(own * 2, 2)]

    def finish(part):
        arrive(share_ref.at[part, pl.ds(1, VISITORS - 1)], share_recv.at[part])

        total_row = sum_out[...]
        for k in range(1, VISITORS):
            total_row = total_row + sums_vmem[k]
        spot = lax.broadcasted_iota(jnp.int32, (HALO, TILE), 1)
        packed = jnp.zeros((HALO, TILE), jnp.float32)
        for n in range(2):
            total = own_ref[part, n]
            for k in range(1, VISITORS):
                total = total + share_ref[part, k, n].astype(jnp.float32)
            weight_sum = jnp.sum(
                jnp.where(lane >> 2 == own * 2 + n, total_row, 0.0), axis=1, keepdims=True
            )
            rows = pl.ds(pl.multiple_of(n * TILE + part * CH, 16), CH)
            weight = prior_vmem[1, rows, :]
            template = (weight * prior_vmem[0, rows, :] + total) / (weight + weight_sum)
            template = template.astype(jnp.bfloat16)
            padded_ref[part, 1 + own * 2 + n, :, :TILE] = template
            wide = template.astype(jnp.float32)
            for h in range(2):
                g = 2 * n + h
                moved = pltpu.roll(
                    wide[h * HALO : (h + 1) * HALO], (2 * HALO * g + HALO) % TILE, 1
                )
                packed = jnp.where(spot >> 5 == g, moved, packed)
        edge_out[part] = packed.astype(jnp.bfloat16)

        @pl.loop(0, VISITORS)
        def _(k):
            for side in range(2):
                edge_copy(part, side, k).start()

        @pl.loop(1, VISITORS)
        def _(k):
            strip_copy(part, k, own).start()

    def wait_strips(part):
        spot = lax.broadcasted_iota(jnp.int32, (HALO, TILE), 1)

        arrive(
            padded_ref.at[part, pl.ds(1, PT - 2), :, pl.ds(0, TILE)], strip_recv.at[part]
        )
        arrive(edge_ref.at[part], edge_recv.at[part])

        @pl.loop(0, VISITORS)
        def _(k):
            left = jnp.where(me > 0, edge_ref[part, 0, k].astype(jnp.float32), 0.0)
            right = jnp.where(me < OWNERS - 1, edge_ref[part, 1, k].astype(jnp.float32), 0.0)
            both = jnp.where(spot & (2 * HALO - 1) < HALO, left, right)
            for g in range(4):
                moved = pltpu.roll(both, (TILE - 2 * HALO * g) % TILE, 1) if g else both
                moved = jnp.where(spot < 2 * HALO, moved, 0.0).astype(jnp.bfloat16)
                n, h = g // 2, g % 2
                padded_ref[
                    part, 1 + earlier(k) * 2 + n, h * HALO : (h + 1) * HALO, TILE:
                ] = moved

    label_local = pltpu.make_async_copy(labels_vmem, labels_ref, local_sem.at[6])

    @pl.loop(0, CHUNKS - 1)
    def _(step):
        gather(step)

        @pl.when(step == 1)
        def _():
            arrive(labels_vmem.at[pl.ds(0, OWNERS - 1)], label_recv)
            label_local.start()
            label_local.wait()

        @pl.when(step == 0)
        def _():
            arrive(sums_vmem.at[pl.ds(1, VISITORS - 1)], sum_recv)

        @pl.when(step > 0)
        def _():
            finish(step - 1)

        @pl.when(step > 1)
        def _():
            wait_strips(step - 2)

    finish(CHUNKS - 2)
    gather(CHUNKS - 1)

    @pl.loop(CHUNKS - 3, CHUNKS - 1)
    def _(part):
        wait_strips(part)

    @pl.loop(0, CHUNKS)
    def _(step):
        part = lax.rem(step + 1, CHUNKS)

        @pl.when(step == 1)
        def _():
            wait_strips(CHUNKS - 1)

        match_chunk(part, padded_ref, down_ref, w_ref, columns_ref, matched_ref)

        @pl.when(step == 0)
        def _():
            finish(CHUNKS - 1)

        @pl.loop(1, OWNERS)
        def _(k):
            to = peer(k)
            for c in range(CAP):
                back_out[part, to, c] = matched_ref[labels_ref[to, 0, me * CAP + c]]
            for q in range(CHUNKS):

                @pl.when(part == q)
                def _():
                    back_copy(q, k, to, me).start()

        for q in range(CHUNKS):

            @pl.when(part == q)
            def _():
                for c in range(CAP):
                    returned[q][me, c] = matched_ref[labels_ref[me, 0, me * CAP + c]]

    written = []
    for step in range(CHUNKS):
        part = (step + 1) % CHUNKS
        rows = pl.ds(part * CH, CH)
        arrive(returned[part].at[pl.ds(0, OWNERS - 1)], back_recv.at[part])

        @pl.loop(0, slots)
        def _(n):
            at = position_ref[n]
            matched = returned[part][at >> 2, at & (CAP - 1)].astype(jnp.float32)
            value = science_ref[n, rows, :].astype(jnp.float32) - matched
            keep = valid_ref[n // PT, n % PT].astype(jnp.float32)
            out_vmem[n, rows, :] = (value * keep).astype(jnp.bfloat16)

        copy = pltpu.make_async_copy(
            out_vmem.at[:, rows, :], out_ref.at[:, rows, :], local_sem.at[10 + part]
        )
        copy.start()
        written.append(copy)

    leave(coefs_vmem.at[pl.ds(0, OWNERS - 1)], coef_send)
    leave(labels_vmem.at[pl.ds(0, OWNERS - 1)], label_send)
    leave(sums_vmem.at[pl.ds(1, VISITORS - 1)], sum_send)
    leave(give_ref.at[:, pl.ds(0, VISITORS - 1)], share_send)
    leave(padded_ref.at[:, pl.ds(1, PT - 2), :, pl.ds(0, TILE)], strip_send)
    leave(edge_ref, edge_send)
    leave(outgoing_ref.at[:, pl.ds(0, OWNERS - 1)], tile_send)
    leave(back_out.at[:, pl.ds(0, OWNERS - 1)], back_send)
    for copy in written:
        copy.wait()


def body(science, tile_ids, valid, weights, kernel_weight_terms, prior_template, prior_weight):
    slots = tile_ids.size
    across, down = band_constants()
    vmem = pl.BlockSpec(memory_space=pltpu.VMEM)
    smem = pl.BlockSpec(memory_space=pltpu.SMEM)
    hbm = pl.BlockSpec(memory_space=pl.ANY)
    dma = pltpu.SemaphoreType.DMA
    f32, bf16, i32 = jnp.float32, jnp.bfloat16, jnp.int32
    result = pl.pallas_call(
        kernel,
        out_shape=jax.ShapeDtypeStruct((slots, TILE, TILE), jnp.bfloat16),
        in_specs=[smem, smem, vmem, vmem, hbm, hbm, hbm, hbm, hbm],
        out_specs=hbm,
        scratch_shapes=[
            pltpu.VMEM((slots, TILE, TILE), bf16),
            pltpu.VMEM((slots, TILE, TILE), bf16),
            pltpu.VMEM(across.shape, bf16),
            pltpu.VMEM(down.shape, bf16),
            pltpu.VMEM((DEEP, GROUP), bf16),
            pltpu.VMEM((PT * CH, DEEP), bf16),
            pltpu.VMEM((CHUNKS, PT + 2, CH, 2 * TILE), bf16),
            pltpu.VMEM((VIS * PT, CH, TILE), bf16),
            pltpu.VMEM((CHUNKS, OWNERS, CAP, CH, TILE), bf16),
            pltpu.VMEM((CHUNKS, OWNERS, CAP, CH, TILE), bf16),
            pltpu.VMEM((OWNERS, CAP, CH, TILE), bf16),
            pltpu.VMEM((OWNERS, CAP, CH, TILE), bf16),
            pltpu.VMEM((OWNERS, CAP, CH, TILE), bf16),
            pltpu.VMEM((OWNERS, CAP, CH, TILE), bf16),
            pltpu.VMEM((CHUNKS, OWNERS, CAP, CH, TILE), bf16),
            pltpu.VMEM((PT, CH, TILE), f32),
            pltpu.VMEM((CHUNKS, 2, CH, TILE), f32),
            pltpu.VMEM((CHUNKS, VISITORS, 2, CH, TILE), bf16),
            pltpu.VMEM((CHUNKS, VISITORS, 2, CH, TILE), bf16),
            pltpu.VMEM((CHUNKS, HALO, TILE), bf16),
            pltpu.VMEM((CHUNKS, 2, VISITORS, HALO, TILE), bf16),
            pltpu.VMEM((2, 2 * TILE, TILE), f32),
            pltpu.VMEM(weights.shape, f32),
            pltpu.VMEM((NPOLY, VIS, NBASIS), f32),
            pltpu.VMEM((1, TILE), i32),
            pltpu.VMEM((1, TILE), i32),
            pltpu.VMEM((OWNERS, 1, TILE), i32),
            pltpu.VMEM((OWNERS, 1, TILE), f32),
            pltpu.VMEM((OWNERS, 1, TILE), f32),
            pltpu.VMEM((1, TILE), f32),
            pltpu.VMEM((VISITORS, 1, TILE), f32),
            pltpu.SMEM(weights.shape, f32),
            pltpu.SMEM((NPOLY, VIS, NBASIS), f32),
            pltpu.SMEM((1, TILE), i32),
            pltpu.SMEM((slots,), i32),
            pltpu.SMEM((OWNERS, 1, TILE), i32),
            pltpu.SMEM((OWNERS, 1, TILE), f32),
            dma((10 + CHUNKS,)),
            dma(()),
            dma(()),
            dma(()),
            dma(()),
            dma(()),
            dma((CHUNKS, (OWNERS - 1) // GATHERED)),
            dma(()),
            dma((CHUNKS,)),
            dma(()),
            dma((CHUNKS,)),
            dma(()),
            dma((CHUNKS,)),
            dma(()),
            dma(()),
            dma(()),
            dma((CHUNKS,)),
        ],
        compiler_params=pltpu.CompilerParams(
            vmem_limit_bytes=56 << 20, collective_id=0, has_side_effects=True
        ),
    )(
        tile_ids,
        valid,
        weights,
        jnp.transpose(kernel_weight_terms, (1, 0, 2)),
        science.reshape(slots, TILE, TILE),
        prior_template,
        prior_weight,
        jnp.asarray(across),
        jnp.asarray(down),
    )
    return result.reshape(science.shape)


def solution(mesh):
    placed = (
        P("visit", "patch", None, None),
        P("visit", "patch"),
        P("visit", "patch"),
        P("visit", "patch"),
        P("visit", None, None),
        P(None, "patch"),
        P(None, "patch"),
    )
    return jax.shard_map(
        body, mesh=mesh, in_specs=placed, out_specs=P("visit", "patch", None, None), check_vma=False
    )
```

```python
import jax
import jax.numpy as jnp
import ml_dtypes
import numpy as np
from jax import lax
from jax.experimental import pallas as pl
from jax.experimental.pallas import tpu as pltpu
from jax.sharding import PartitionSpec as P

TILE = 128
KHALF = 15
HALO = 16
SPAN = TILE + 2 * HALO
SIGMAS = (1.5, 3.0, 5.0, 7.0)
DEGREES = (4, 2, 1, 0)
NPROF = 11
NBASIS = 25
NPOLY = 6
PT = 16
SKY = 2048
VIS = 2
GROUP = 3 * VIS * TILE
CH = 32
CHUNKS = TILE // CH
MAIN = NPROF * TILE
DEEP = MAIN + 3 * TILE
OWNERS = 16
VISITORS = 8
CAP = 4
GATHERED = 5
GROUPS = (OWNERS - 1) // GATHERED
AHEAD = 4
MESH = pl.DeviceIdType.MESH


def profile_table():
    u = np.arange(-KHALF, KHALF + 1, dtype=np.float32)
    rows = []
    for sigma, degree in zip(SIGMAS, DEGREES):
        scaled = u / np.float32(sigma)
        envelope = np.exp(np.float32(-0.5) * scaled * scaled)
        for power in range(degree + 1):
            shaped = envelope * scaled**power
            rows.append(shaped / np.sum(np.abs(shaped)))
    return np.stack(rows).astype(np.float32)


def band_constants():
    profiles = profile_table()
    target = np.arange(TILE)

    def band(source):
        taps = source[:, None] - target[None, :] + KHALF
        inside = (taps >= 0) & (taps <= 2 * KHALF)
        return np.where(inside[None], profiles[:, np.clip(taps, 0, 2 * KHALF)], 0.0)

    columns = np.concatenate(
        [np.arange(TILE), np.arange(-HALO, 0), np.arange(TILE, TILE + HALO)]
    )
    across = band(columns).astype(ml_dtypes.bfloat16)
    down = band(np.arange(-HALO, CH + HALO))[:, :, :CH].transpose(0, 2, 1)
    down = down.reshape(NPROF * CH, CH + 2 * HALO).astype(ml_dtypes.bfloat16)
    return across, down


def basis_order():
    order, start = [], 0
    for degree in DEGREES:
        for j in range(degree + 1):
            order.append((start + j, [start + i for i in range(degree - j + 1)]))
        start += degree + 1
    return order


def build_weights(strip, kw_ref, across_ref, w_ref):
    lane = lax.broadcasted_iota(jnp.int32, (1, TILE), 1) + strip * TILE
    x = (lane.astype(jnp.float32) + 0.5) / SKY * 2.0 - 1.0
    xx = x * x
    unused = MAIN + NPROF * 2 * HALO
    w_ref[unused:, :] = jnp.zeros((DEEP - unused, GROUP), jnp.bfloat16)
    k = 0
    for j, sources in basis_order():
        for v in range(VIS):
            sums = [None, None, None]
            for n, source in enumerate(sources):
                c = [kw_ref[m, v, k + n] for m in range(NPOLY)]
                rows = (c[0] + c[1] * x + c[3] * xx, c[2] + c[4] * x, c[5])
                image = across_ref[source].astype(jnp.float32)
                for b in range(3):
                    term = rows[b] * image
                    sums[b] = term if sums[b] is None else sums[b] + term
            for b in range(3):
                at = (b * VIS + v) * TILE
                value = sums[b].astype(jnp.bfloat16)
                halo = MAIN + j * 2 * HALO
                w_ref[j * TILE : (j + 1) * TILE, at : at + TILE] = value[:TILE]
                w_ref[halo : halo + 2 * HALO, at : at + TILE] = value[TILE:]
        k += len(sources)


def match_chunk(part, padded_ref, down_ref, w_ref, columns_ref, matched_ref):
    first = (part == 0).astype(jnp.int32)
    last = (part == CHUNKS - 1).astype(jnp.int32)
    before = lax.rem(part + CHUNKS - 1, CHUNKS)
    after = lax.rem(part + 1, CHUNKS)

    @pl.loop(0, PT, unroll=True)
    def _(tile):
        rows = pl.ds(pl.multiple_of(tile * CH, 16), CH)
        window = jnp.concatenate(
            [
                padded_ref[before, tile + 1 - first, CH - HALO :, :],
                padded_ref[part, tile + 1],
                padded_ref[after, tile + 1 + last, :HALO, :],
            ],
            axis=0,
        )
        both = jnp.dot(down_ref[...], window, preferred_element_type=jnp.float32)
        for group in range(3):
            total = None
            for q in range(min(4, NPROF - 4 * group)):
                j = 4 * group + q
                piece = both[j * CH : (j + 1) * CH]
                columns_ref[rows, j * TILE : (j + 1) * TILE] = piece[:, :TILE].astype(jnp.bfloat16)
                side = piece[:, TILE:]
                side = pltpu.roll(side, 2 * HALO * q, 1) if q else side
                total = side if total is None else total + side
            at = MAIN + group * TILE
            columns_ref[rows, at : at + TILE] = total.astype(jnp.bfloat16)

    half = VIS * TILE
    line = lax.broadcasted_iota(jnp.int32, (PT * CH, 1), 0)
    y = ((line >> 5) * TILE + part * CH + (line & (CH - 1))).astype(jnp.float32)
    y = (y + 0.5) / SKY * 2.0 - 1.0
    total = jnp.zeros((PT * CH, half), jnp.float32)
    for power, factor in enumerate((None, y, y * y)):
        term = jnp.dot(
            columns_ref[...],
            w_ref[:, power * half : (power + 1) * half],
            preferred_element_type=jnp.float32,
        )
        total = total + (term if factor is None else factor * term)
    total = total.astype(jnp.bfloat16)
    for v in range(VIS):
        for tile in range(PT):
            matched_ref[v * PT + tile] = total[
                tile * CH : (tile + 1) * CH, v * TILE : (v + 1) * TILE
            ]


def remote(src, dst, send, recv, visit, patch):
    return pltpu.make_async_remote_copy(
        src_ref=src,
        dst_ref=dst,
        send_sem=send,
        recv_sem=recv,
        device_id={"visit": visit, "patch": patch},
        device_id_type=MESH,
    )


def kernel(
    ids_ref, valid_ref, weights_ref, terms_ref, science_hbm,
    prior_ref, prior_weight_ref, across_hbm, down_hbm, out_ref,
    out_vmem, science_ref, across_ref, down_ref,
    w_ref, columns_ref, padded_ref, matched_ref, outgoing_ref, arrived_ref,
    back_0, back_1, back_2, back_3,
    back_out, acc_ref, own_ref, give_ref, share_ref, edge_out, edge_ref, prior_vmem,
    slot_weight_vmem, terms_vmem, source_vmem, label_out, labels_vmem, coef_out, coefs_vmem,
    sum_out, sums_vmem,
    slot_weight_ref, kw_ref, source_ref, position_ref, labels_ref, coef_ref,
    local_sem, label_send, label_recv, coef_send, coef_recv, tile_send, tile_recv,
    share_send, share_recv, strip_send, strip_recv, edge_send, edge_recv,
    sum_send, sum_recv, back_send, back_recv,
):
    visit = lax.axis_index("visit")
    me = lax.axis_index("patch")
    own = visit
    returned = (back_0, back_1, back_2, back_3)
    slots = VIS * PT

    def peer(k):
        return lax.rem(me + k, OWNERS)

    def origin(k):
        return lax.rem(me + OWNERS - k, OWNERS)

    def other(k):
        return lax.rem(visit + k, VISITORS)

    def earlier(k):
        return lax.rem(visit + VISITORS - k, VISITORS)

    def neighbour(side):
        return peer(1) if side == 0 else origin(1)

    science_copy = pltpu.make_async_copy(science_hbm, science_ref, local_sem.at[7])
    across_copy = pltpu.make_async_copy(across_hbm, across_ref, local_sem.at[8])
    down_copy = pltpu.make_async_copy(down_hbm, down_ref, local_sem.at[9])
    science_copy.start()
    barrier = pltpu.get_barrier_semaphore()

    def greet(to_visit, to_patch):
        pl.semaphore_signal(
            barrier, inc=1, device_id={"visit": to_visit, "patch": to_patch}, device_id_type=MESH
        )

    @pl.loop(1, OWNERS)
    def _(k):
        greet(visit, peer(k))

    @pl.loop(1, VISITORS)
    def _(k):
        greet(other(k), me)
        greet(other(k), peer(1))
        greet(other(k), origin(1))

    prior_copies = [
        pltpu.make_async_copy(
            ref.at[pl.ds(pl.multiple_of(own * 256, 256), 256), :],
            prior_vmem.at[n],
            local_sem.at[n],
        )
        for n, ref in enumerate((prior_ref, prior_weight_ref))
    ]
    for copy in prior_copies:
        copy.start()
    across_copy.start()
    down_copy.start()
    slot_weight_vmem[...] = weights_ref[...].astype(jnp.float32)
    terms_vmem[...] = terms_ref[...].astype(jnp.float32)
    weight_copy = pltpu.make_async_copy(slot_weight_vmem, slot_weight_ref, local_sem.at[2])
    terms_copy = pltpu.make_async_copy(terms_vmem, kw_ref, local_sem.at[3])
    weight_copy.start()
    terms_copy.start()

    ids = [ids_ref[n // PT, n % PT] for n in range(slots)]
    strips = [value >> 4 for value in ids]
    tiles = [value & (PT - 1) for value in ids]
    for n in range(slots):
        rank = 0
        for m in range(n):
            rank = rank + jnp.where(strips[m] == strips[n], 1, 0)
        position_ref[n] = strips[n] * CAP + rank

    lane = lax.broadcasted_iota(jnp.int32, (1, TILE), 1)
    source = jnp.zeros((1, TILE), jnp.int32)
    label = jnp.zeros((1, TILE), jnp.int32)
    for n in range(slots):
        here = lane == position_ref[n]
        source = jnp.where(here, n, source)
        label = jnp.where(here, n // PT * PT + tiles[n], label)
    source_vmem[...] = source
    label_out[...] = label
    source_copy = pltpu.make_async_copy(source_vmem, source_ref, local_sem.at[4])
    source_copy.start()
    weight_copy.wait()
    owner_row = lax.broadcasted_iota(jnp.int32, (OWNERS, TILE), 0)
    entry = lax.broadcasted_iota(jnp.int32, (OWNERS, TILE), 1)
    coefs = jnp.zeros((OWNERS, TILE), jnp.float32)
    for n in range(slots):
        v, s = n // PT, n % PT
        at = position_ref[n]
        here = (owner_row == at >> 2) & (entry == tiles[n] * CAP + (at & (CAP - 1)))
        weight = slot_weight_ref[v, s] * valid_ref[v, s].astype(jnp.float32)
        coefs = jnp.where(here, weight, coefs)
    for to in range(OWNERS):
        coef_out[to] = coefs[to : to + 1]
    source_copy.wait()
    terms_copy.wait()
    science_copy.wait()

    pl.semaphore_wait(barrier, OWNERS - 1 + 3 * (VISITORS - 1))

    def coef_copy(k, to, slot):
        return remote(
            coef_out.at[to], coefs_vmem.at[slot], coef_send, coef_recv, visit, to
        )

    def label_copy(k, to, slot):
        return remote(
            label_out, labels_vmem.at[slot], label_send, label_recv, visit, to
        )

    def tile_copy(part, k, to, slot):
        return remote(
            outgoing_ref.at[part, to], arrived_ref.at[part, slot],
            tile_send, tile_recv.at[part, (k - 1) // GATHERED], visit, to,
        )

    def back_copy(part, k, to, slot):
        return remote(
            back_out.at[part, to], returned[part].at[slot],
            back_send, back_recv.at[part], visit, to,
        )

    def arrive(block, semaphore):
        remote(block, block, semaphore, semaphore, visit, peer(1)).wait_recv()

    def leave(block, semaphore):
        remote(block, block, semaphore, semaphore, visit, peer(1)).wait_send()

    def sum_copy(k):
        return remote(sum_out, sums_vmem.at[k], sum_send, sum_recv, other(k), me)

    def share_copy(part, k):
        return remote(
            give_ref.at[part, other(k)], share_ref.at[part, k],
            share_send, share_recv.at[part], other(k), me,
        )

    def strip_copy(part, k, owner):
        rows = padded_ref.at[part, pl.ds(1 + 2 * owner, 2), :, pl.ds(0, TILE)]
        return remote(rows, rows, strip_send, strip_recv.at[part], other(k), me)

    def edge_copy(part, side, k):
        return remote(
            edge_out.at[part], edge_ref.at[part, side, k],
            edge_send, edge_recv.at[part], other(k), neighbour(side),
        )

    def pack(part, to, target, at):
        rows = pl.ds(pl.multiple_of(part * CH, 16), CH)
        for c in range(CAP):
            target[part, at, c] = science_ref[source_ref[0, to * CAP + c], rows, :]

    @pl.loop(1, OWNERS)
    def _(k):
        coef_copy(k, peer(k), me).start()
        label_copy(k, peer(k), me).start()

    def send_tiles(batch):
        part = batch // GROUPS

        @pl.loop(1, GATHERED + 1)
        def _(n):
            k = (batch % GROUPS) * GATHERED + n
            pack(part, peer(k), outgoing_ref, peer(k))
            tile_copy(part, k, peer(k), me).start()

    @pl.loop(0, AHEAD)
    def _(batch):
        send_tiles(batch)

    @pl.loop(0, CHUNKS)
    def _(part):
        pack(part, me, arrived_ref, me)

    labels_vmem[me] = label_out[...]
    coefs_vmem[me] = coef_out[me]

    arrive(coefs_vmem.at[pl.ds(0, OWNERS - 1)], coef_recv)

    coef_local = pltpu.make_async_copy(coefs_vmem, coef_ref, local_sem.at[5])
    coef_local.start()
    row = coefs_vmem[0]
    for at in range(1, OWNERS):
        row = row + coefs_vmem[at]
    sum_out[...] = row

    @pl.loop(1, VISITORS)
    def _(k):
        sum_copy(k).start()

    across_copy.wait()
    down_copy.wait()
    build_weights(me, kw_ref, across_ref, w_ref)
    blank = jnp.zeros((CH, 2 * TILE), jnp.bfloat16)
    for part in range(CHUNKS):
        padded_ref[part, 0] = blank
        padded_ref[part, PT + 1] = blank
    for copy in prior_copies:
        copy.wait()
    coef_local.wait()

    def add_slots(part, at, fresh):
        tiles = [arrived_ref[part, at, c].astype(jnp.float32) for c in range(CAP)]
        for t in range(PT):
            value = None if fresh else acc_ref[t]
            for c in range(CAP):
                term = coef_ref[at, 0, t * CAP + c] * tiles[c]
                value = term if value is None else value + term
            acc_ref[t] = value

    def gather(part):
        add_slots(part, me, True)

        @pl.loop(0, (OWNERS - 1) // GATHERED)
        def _(group):
            arrive(arrived_ref.at[part, pl.ds(0, GATHERED)], tile_recv.at[part, group])
            batch = part * GROUPS + group + AHEAD

            @pl.when(batch < CHUNKS * GROUPS)
            def _():
                send_tiles(batch)

            @pl.loop(1, GATHERED + 1)
            def _(k):
                add_slots(part, origin(group * GATHERED + k), False)

        for to in range(VISITORS):
            for n in range(2):
                give_ref[part, to, n] = acc_ref[2 * to + n].astype(jnp.bfloat16)

        @pl.loop(1, VISITORS)
        def _(k):
            share_copy(part, k).start()

        own_ref[part] = acc_ref[pl.ds(own * 2, 2)]

    def finish(part):
        arrive(share_ref.at[part, pl.ds(1, VISITORS - 1)], share_recv.at[part])

        total_row = sum_out[...]
        for k in range(1, VISITORS):
            total_row = total_row + sums_vmem[k]
        spot = lax.broadcasted_iota(jnp.int32, (HALO, TILE), 1)
        packed = jnp.zeros((HALO, TILE), jnp.float32)
        for n in range(2):
            total = own_ref[part, n]
            for k in range(1, VISITORS):
                total = total + share_ref[part, k, n].astype(jnp.float32)
            weight_sum = jnp.sum(
                jnp.where(lane >> 2 == own * 2 + n, total_row, 0.0), axis=1, keepdims=True
            )
            rows = pl.ds(pl.multiple_of(n * TILE + part * CH, 16), CH)
            weight = prior_vmem[1, rows, :]
            template = (weight * prior_vmem[0, rows, :] + total) / (weight + weight_sum)
            template = template.astype(jnp.bfloat16)
            padded_ref[part, 1 + own * 2 + n, :, :TILE] = template
            wide = template.astype(jnp.float32)
            for h in range(2):
                g = 2 * n + h
                moved = pltpu.roll(
                    wide[h * HALO : (h + 1) * HALO], (2 * HALO * g + HALO) % TILE, 1
                )
                packed = jnp.where(spot >> 5 == g, moved, packed)
        edge_out[part] = packed.astype(jnp.bfloat16)

        @pl.loop(0, VISITORS)
        def _(k):
            for side in range(2):
                edge_copy(part, side, k).start()

        @pl.loop(1, VISITORS)
        def _(k):
            strip_copy(part, k, own).start()

    def wait_strips(part):
        spot = lax.broadcasted_iota(jnp.int32, (HALO, TILE), 1)

        arrive(
            padded_ref.at[part, pl.ds(1, PT - 2), :, pl.ds(0, TILE)], strip_recv.at[part]
        )
        arrive(edge_ref.at[part], edge_recv.at[part])

        @pl.loop(0, VISITORS)
        def _(k):
            left = jnp.where(me > 0, edge_ref[part, 0, k].astype(jnp.float32), 0.0)
            right = jnp.where(me < OWNERS - 1, edge_ref[part, 1, k].astype(jnp.float32), 0.0)
            both = jnp.where(spot & (2 * HALO - 1) < HALO, left, right)
            for g in range(4):
                moved = pltpu.roll(both, (TILE - 2 * HALO * g) % TILE, 1) if g else both
                moved = jnp.where(spot < 2 * HALO, moved, 0.0).astype(jnp.bfloat16)
                n, h = g // 2, g % 2
                padded_ref[
                    part, 1 + earlier(k) * 2 + n, h * HALO : (h + 1) * HALO, TILE:
                ] = moved

    label_local = pltpu.make_async_copy(labels_vmem, labels_ref, local_sem.at[6])

    @pl.loop(0, CHUNKS - 1)
    def _(step):
        gather(step)

        @pl.when(step == 1)
        def _():
            arrive(labels_vmem.at[pl.ds(0, OWNERS - 1)], label_recv)
            label_local.start()
            label_local.wait()

        @pl.when(step == 0)
        def _():
            arrive(sums_vmem.at[pl.ds(1, VISITORS - 1)], sum_recv)

        @pl.when(step > 0)
        def _():
            finish(step - 1)

        @pl.when(step > 1)
        def _():
            wait_strips(step - 2)

    finish(CHUNKS - 2)
    gather(CHUNKS - 1)

    @pl.loop(CHUNKS - 3, CHUNKS - 1)
    def _(part):
        wait_strips(part)

    @pl.loop(0, CHUNKS)
    def _(step):
        part = lax.rem(step + 1, CHUNKS)

        @pl.when(step == 1)
        def _():
            wait_strips(CHUNKS - 1)

        match_chunk(part, padded_ref, down_ref, w_ref, columns_ref, matched_ref)

        @pl.when(step == 0)
        def _():
            finish(CHUNKS - 1)

        @pl.loop(1, OWNERS)
        def _(k):
            to = peer(k)
            for c in range(CAP):
                back_out[part, to, c] = matched_ref[labels_ref[to, 0, me * CAP + c]]
            for q in range(CHUNKS):

                @pl.when(part == q)
                def _():
                    back_copy(q, k, to, me).start()

        for q in range(CHUNKS):

            @pl.when(part == q)
            def _():
                for c in range(CAP):
                    returned[q][me, c] = matched_ref[labels_ref[me, 0, me * CAP + c]]

    written = []
    for step in range(CHUNKS):
        part = (step + 1) % CHUNKS
        rows = pl.ds(part * CH, CH)
        arrive(returned[part].at[pl.ds(0, OWNERS - 1)], back_recv.at[part])

        @pl.loop(0, slots)
        def _(n):
            at = position_ref[n]
            matched = returned[part][at >> 2, at & (CAP - 1)].astype(jnp.float32)
            value = science_ref[n, rows, :].astype(jnp.float32) - matched
            keep = valid_ref[n // PT, n % PT].astype(jnp.float32)
            out_vmem[n, rows, :] = (value * keep).astype(jnp.bfloat16)

        copy = pltpu.make_async_copy(
            out_vmem.at[:, rows, :], out_ref.at[:, rows, :], local_sem.at[10 + part]
        )
        copy.start()
        written.append(copy)

    leave(coefs_vmem.at[pl.ds(0, OWNERS - 1)], coef_send)
    leave(labels_vmem.at[pl.ds(0, OWNERS - 1)], label_send)
    leave(sums_vmem.at[pl.ds(1, VISITORS - 1)], sum_send)
    leave(give_ref.at[:, pl.ds(0, VISITORS - 1)], share_send)
    leave(padded_ref.at[:, pl.ds(1, PT - 2), :, pl.ds(0, TILE)], strip_send)
    leave(edge_ref, edge_send)
    leave(outgoing_ref.at[:, pl.ds(0, OWNERS - 1)], tile_send)
    leave(back_out.at[:, pl.ds(0, OWNERS - 1)], back_send)
    for copy in written:
        copy.wait()


def body(science, tile_ids, valid, weights, kernel_weight_terms, prior_template, prior_weight):
    slots = tile_ids.size
    across, down = band_constants()
    vmem = pl.BlockSpec(memory_space=pltpu.VMEM)
    smem = pl.BlockSpec(memory_space=pltpu.SMEM)
    hbm = pl.BlockSpec(memory_space=pl.ANY)
    dma = pltpu.SemaphoreType.DMA
    f32, bf16, i32 = jnp.float32, jnp.bfloat16, jnp.int32
    result = pl.pallas_call(
        kernel,
        out_shape=jax.ShapeDtypeStruct((slots, TILE, TILE), jnp.bfloat16),
        in_specs=[smem, smem, vmem, vmem, hbm, hbm, hbm, hbm, hbm],
        out_specs=hbm,
        scratch_shapes=[
            pltpu.VMEM((slots, TILE, TILE), bf16),
            pltpu.VMEM((slots, TILE, TILE), bf16),
            pltpu.VMEM(across.shape, bf16),
            pltpu.VMEM(down.shape, bf16),
            pltpu.VMEM((DEEP, GROUP), bf16),
            pltpu.VMEM((PT * CH, DEEP), bf16),
            pltpu.VMEM((CHUNKS, PT + 2, CH, 2 * TILE), bf16),
            pltpu.VMEM((VIS * PT, CH, TILE), bf16),
            pltpu.VMEM((CHUNKS, OWNERS, CAP, CH, TILE), bf16),
            pltpu.VMEM((CHUNKS, OWNERS, CAP, CH, TILE), bf16),
            pltpu.VMEM((OWNERS, CAP, CH, TILE), bf16),
            pltpu.VMEM((OWNERS, CAP, CH, TILE), bf16),
            pltpu.VMEM((OWNERS, CAP, CH, TILE), bf16),
            pltpu.VMEM((OWNERS, CAP, CH, TILE), bf16),
            pltpu.VMEM((CHUNKS, OWNERS, CAP, CH, TILE), bf16),
            pltpu.VMEM((PT, CH, TILE), f32),
            pltpu.VMEM((CHUNKS, 2, CH, TILE), f32),
            pltpu.VMEM((CHUNKS, VISITORS, 2, CH, TILE), bf16),
            pltpu.VMEM((CHUNKS, VISITORS, 2, CH, TILE), bf16),
            pltpu.VMEM((CHUNKS, HALO, TILE), bf16),
            pltpu.VMEM((CHUNKS, 2, VISITORS, HALO, TILE), bf16),
            pltpu.VMEM((2, 2 * TILE, TILE), f32),
            pltpu.VMEM(weights.shape, f32),
            pltpu.VMEM((NPOLY, VIS, NBASIS), f32),
            pltpu.VMEM((1, TILE), i32),
            pltpu.VMEM((1, TILE), i32),
            pltpu.VMEM((OWNERS, 1, TILE), i32),
            pltpu.VMEM((OWNERS, 1, TILE), f32),
            pltpu.VMEM((OWNERS, 1, TILE), f32),
            pltpu.VMEM((1, TILE), f32),
            pltpu.VMEM((VISITORS, 1, TILE), f32),
            pltpu.SMEM(weights.shape, f32),
            pltpu.SMEM((NPOLY, VIS, NBASIS), f32),
            pltpu.SMEM((1, TILE), i32),
            pltpu.SMEM((slots,), i32),
            pltpu.SMEM((OWNERS, 1, TILE), i32),
            pltpu.SMEM((OWNERS, 1, TILE), f32),
            dma((10 + CHUNKS,)),
            dma(()),
            dma(()),
            dma(()),
            dma(()),
            dma(()),
            dma((CHUNKS, (OWNERS - 1) // GATHERED)),
            dma(()),
            dma((CHUNKS,)),
            dma(()),
            dma((CHUNKS,)),
            dma(()),
            dma((CHUNKS,)),
            dma(()),
            dma(()),
            dma(()),
            dma((CHUNKS,)),
        ],
        compiler_params=pltpu.CompilerParams(
            vmem_limit_bytes=56 << 20, collective_id=0, has_side_effects=True
        ),
    )(
        tile_ids,
        valid,
        weights,
        jnp.transpose(kernel_weight_terms, (1, 0, 2)),
        science.reshape(slots, TILE, TILE),
        prior_template,
        prior_weight,
        jnp.asarray(across),
        jnp.asarray(down),
    )
    return result.reshape(science.shape)


def solution(mesh):
    placed = (
        P("visit", "patch", None, None),
        P("visit", "patch"),
        P("visit", "patch"),
        P("visit", "patch"),
        P("visit", None, None),
        P(None, "patch"),
        P(None, "patch"),
    )
    return jax.shard_map(
        body, mesh=mesh, in_specs=placed, out_specs=P("visit", "patch", None, None), check_vma=False
    )
```

```python
import jax
import jax.numpy as jnp
import ml_dtypes
import numpy as np
from jax import lax
from jax.experimental import pallas as pl
from jax.experimental.pallas import tpu as pltpu
from jax.sharding import PartitionSpec as P

TILE = 128
KHALF = 15
HALO = 16
SPAN = TILE + 2 * HALO
SIGMAS = (1.5, 3.0, 5.0, 7.0)
DEGREES = (4, 2, 1, 0)
NPROF = 11
NBASIS = 25
NPOLY = 6
PT = 16
SKY = 2048
VIS = 2
GROUP = 3 * VIS * TILE
CH = 32
CHUNKS = TILE // CH
MAIN = NPROF * TILE
DEEP = MAIN + 3 * TILE
OWNERS = 16
VISITORS = 8
CAP = 4
GATHERED = 3
GROUPS = (OWNERS - 1) // GATHERED
AHEAD = 7
MESH = pl.DeviceIdType.MESH


def profile_table():
    u = np.arange(-KHALF, KHALF + 1, dtype=np.float32)
    rows = []
    for sigma, degree in zip(SIGMAS, DEGREES):
        scaled = u / np.float32(sigma)
        envelope = np.exp(np.float32(-0.5) * scaled * scaled)
        for power in range(degree + 1):
            shaped = envelope * scaled**power
            rows.append(shaped / np.sum(np.abs(shaped)))
    return np.stack(rows).astype(np.float32)


def band_constants():
    profiles = profile_table()
    target = np.arange(TILE)

    def band(source):
        taps = source[:, None] - target[None, :] + KHALF
        inside = (taps >= 0) & (taps <= 2 * KHALF)
        return np.where(inside[None], profiles[:, np.clip(taps, 0, 2 * KHALF)], 0.0)

    columns = np.concatenate(
        [np.arange(TILE), np.arange(-HALO, 0), np.arange(TILE, TILE + HALO)]
    )
    across = band(columns).astype(ml_dtypes.bfloat16)
    down = band(np.arange(-HALO, CH + HALO))[:, :, :CH].transpose(0, 2, 1)
    down = down.reshape(NPROF * CH, CH + 2 * HALO).astype(ml_dtypes.bfloat16)
    return across, down


def basis_order():
    order, start = [], 0
    for degree in DEGREES:
        for j in range(degree + 1):
            order.append((start + j, [start + i for i in range(degree - j + 1)]))
        start += degree + 1
    return order


def build_weights(strip, kw_ref, across_ref, w_ref):
    lane = lax.broadcasted_iota(jnp.int32, (1, TILE), 1) + strip * TILE
    x = (lane.astype(jnp.float32) + 0.5) / SKY * 2.0 - 1.0
    xx = x * x
    unused = MAIN + NPROF * 2 * HALO
    w_ref[unused:, :] = jnp.zeros((DEEP - unused, GROUP), jnp.bfloat16)
    k = 0
    for j, sources in basis_order():
        for v in range(VIS):
            sums = [None, None, None]
            for n, source in enumerate(sources):
                c = [kw_ref[m, v, k + n] for m in range(NPOLY)]
                rows = (c[0] + c[1] * x + c[3] * xx, c[2] + c[4] * x, c[5])
                image = across_ref[source].astype(jnp.float32)
                for b in range(3):
                    term = rows[b] * image
                    sums[b] = term if sums[b] is None else sums[b] + term
            for b in range(3):
                at = (b * VIS + v) * TILE
                value = sums[b].astype(jnp.bfloat16)
                halo = MAIN + j * 2 * HALO
                w_ref[j * TILE : (j + 1) * TILE, at : at + TILE] = value[:TILE]
                w_ref[halo : halo + 2 * HALO, at : at + TILE] = value[TILE:]
        k += len(sources)


def match_chunk(part, padded_ref, down_ref, w_ref, columns_ref, matched_ref):
    first = (part == 0).astype(jnp.int32)
    last = (part == CHUNKS - 1).astype(jnp.int32)
    before = lax.rem(part + CHUNKS - 1, CHUNKS)
    after = lax.rem(part + 1, CHUNKS)

    @pl.loop(0, PT, unroll=True)
    def _(tile):
        rows = pl.ds(pl.multiple_of(tile * CH, 16), CH)
        window = jnp.concatenate(
            [
                padded_ref[before, tile + 1 - first, CH - HALO :, :],
                padded_ref[part, tile + 1],
                padded_ref[after, tile + 1 + last, :HALO, :],
            ],
            axis=0,
        )
        both = jnp.dot(down_ref[...], window, preferred_element_type=jnp.float32)
        for group in range(3):
            total = None
            for q in range(min(4, NPROF - 4 * group)):
                j = 4 * group + q
                piece = both[j * CH : (j + 1) * CH]
                columns_ref[rows, j * TILE : (j + 1) * TILE] = piece[:, :TILE].astype(jnp.bfloat16)
                side = piece[:, TILE:]
                side = pltpu.roll(side, 2 * HALO * q, 1) if q else side
                total = side if total is None else total + side
            at = MAIN + group * TILE
            columns_ref[rows, at : at + TILE] = total.astype(jnp.bfloat16)

    half = VIS * TILE
    line = lax.broadcasted_iota(jnp.int32, (PT * CH, 1), 0)
    y = ((line >> 5) * TILE + part * CH + (line & (CH - 1))).astype(jnp.float32)
    y = (y + 0.5) / SKY * 2.0 - 1.0
    total = jnp.zeros((PT * CH, half), jnp.float32)
    for power, factor in enumerate((None, y, y * y)):
        term = jnp.dot(
            columns_ref[...],
            w_ref[:, power * half : (power + 1) * half],
            preferred_element_type=jnp.float32,
        )
        total = total + (term if factor is None else factor * term)
    total = total.astype(jnp.bfloat16)
    for v in range(VIS):
        for tile in range(PT):
            matched_ref[v * PT + tile] = total[
                tile * CH : (tile + 1) * CH, v * TILE : (v + 1) * TILE
            ]


def remote(src, dst, send, recv, visit, patch):
    return pltpu.make_async_remote_copy(
        src_ref=src,
        dst_ref=dst,
        send_sem=send,
        recv_sem=recv,
        device_id={"visit": visit, "patch": patch},
        device_id_type=MESH,
    )


def kernel(
    ids_ref, valid_ref, weights_ref, terms_ref, science_hbm,
    prior_ref, prior_weight_ref, across_hbm, down_hbm, out_ref,
    out_vmem, science_ref, across_ref, down_ref,
    w_ref, columns_ref, padded_ref, matched_ref, outgoing_ref, arrived_ref,
    back_0, back_1, back_2, back_3,
    back_out, acc_ref, own_ref, give_ref, share_ref, edge_out, edge_ref, prior_vmem,
    slot_weight_vmem, terms_vmem, source_vmem, label_out, labels_vmem, coef_out, coefs_vmem,
    sum_out, sums_vmem,
    slot_weight_ref, kw_ref, source_ref, position_ref, labels_ref, coef_ref,
    local_sem, label_send, label_recv, coef_send, coef_recv, tile_send, tile_recv,
    share_send, share_recv, strip_send, strip_recv, edge_send, edge_recv,
    sum_send, sum_recv, back_send, back_recv,
):
    visit = lax.axis_index("visit")
    me = lax.axis_index("patch")
    own = visit
    returned = (back_0, back_1, back_2, back_3)
    slots = VIS * PT

    def peer(k):
        return lax.rem(me + k, OWNERS)

    def origin(k):
        return lax.rem(me + OWNERS - k, OWNERS)

    def other(k):
        return lax.rem(visit + k, VISITORS)

    def earlier(k):
        return lax.rem(visit + VISITORS - k, VISITORS)

    def neighbour(side):
        return peer(1) if side == 0 else origin(1)

    science_copy = pltpu.make_async_copy(science_hbm, science_ref, local_sem.at[7])
    across_copy = pltpu.make_async_copy(across_hbm, across_ref, local_sem.at[8])
    down_copy = pltpu.make_async_copy(down_hbm, down_ref, local_sem.at[9])
    science_copy.start()
    barrier = pltpu.get_barrier_semaphore()

    def greet(to_visit, to_patch):
        pl.semaphore_signal(
            barrier, inc=1, device_id={"visit": to_visit, "patch": to_patch}, device_id_type=MESH
        )

    @pl.loop(1, OWNERS)
    def _(k):
        greet(visit, peer(k))

    @pl.loop(1, VISITORS)
    def _(k):
        greet(other(k), me)
        greet(other(k), peer(1))
        greet(other(k), origin(1))

    prior_copies = [
        pltpu.make_async_copy(
            ref.at[pl.ds(pl.multiple_of(own * 256, 256), 256), :],
            prior_vmem.at[n],
            local_sem.at[n],
        )
        for n, ref in enumerate((prior_ref, prior_weight_ref))
    ]
    for copy in prior_copies:
        copy.start()
    across_copy.start()
    down_copy.start()
    slot_weight_vmem[...] = weights_ref[...].astype(jnp.float32)
    terms_vmem[...] = terms_ref[...].astype(jnp.float32)
    weight_copy = pltpu.make_async_copy(slot_weight_vmem, slot_weight_ref, local_sem.at[2])
    terms_copy = pltpu.make_async_copy(terms_vmem, kw_ref, local_sem.at[3])
    weight_copy.start()
    terms_copy.start()

    ids = [ids_ref[n // PT, n % PT] for n in range(slots)]
    strips = [value >> 4 for value in ids]
    tiles = [value & (PT - 1) for value in ids]
    for n in range(slots):
        rank = 0
        for m in range(n):
            rank = rank + jnp.where(strips[m] == strips[n], 1, 0)
        position_ref[n] = strips[n] * CAP + rank

    lane = lax.broadcasted_iota(jnp.int32, (1, TILE), 1)
    source = jnp.zeros((1, TILE), jnp.int32)
    label = jnp.zeros((1, TILE), jnp.int32)
    for n in range(slots):
        here = lane == position_ref[n]
        source = jnp.where(here, n, source)
        label = jnp.where(here, n // PT * PT + tiles[n], label)
    source_vmem[...] = source
    label_out[...] = label
    source_copy = pltpu.make_async_copy(source_vmem, source_ref, local_sem.at[4])
    source_copy.start()
    weight_copy.wait()
    owner_row = lax.broadcasted_iota(jnp.int32, (OWNERS, TILE), 0)
    entry = lax.broadcasted_iota(jnp.int32, (OWNERS, TILE), 1)
    coefs = jnp.zeros((OWNERS, TILE), jnp.float32)
    for n in range(slots):
        v, s = n // PT, n % PT
        at = position_ref[n]
        here = (owner_row == at >> 2) & (entry == tiles[n] * CAP + (at & (CAP - 1)))
        weight = slot_weight_ref[v, s] * valid_ref[v, s].astype(jnp.float32)
        coefs = jnp.where(here, weight, coefs)
    for to in range(OWNERS):
        coef_out[to] = coefs[to : to + 1]
    source_copy.wait()
    terms_copy.wait()
    science_copy.wait()

    pl.semaphore_wait(barrier, OWNERS - 1 + 3 * (VISITORS - 1))

    def coef_copy(k, to, slot):
        return remote(
            coef_out.at[to], coefs_vmem.at[slot], coef_send, coef_recv, visit, to
        )

    def label_copy(k, to, slot):
        return remote(
            label_out, labels_vmem.at[slot], label_send, label_recv, visit, to
        )

    def tile_copy(part, k, to, slot):
        return remote(
            outgoing_ref.at[part, to], arrived_ref.at[part, slot],
            tile_send, tile_recv.at[part, (k - 1) // GATHERED], visit, to,
        )

    def back_copy(part, k, to, slot):
        return remote(
            back_out.at[part, to], returned[part].at[slot],
            back_send, back_recv.at[part], visit, to,
        )

    def arrive(block, semaphore):
        remote(block, block, semaphore, semaphore, visit, peer(1)).wait_recv()

    def leave(block, semaphore):
        remote(block, block, semaphore, semaphore, visit, peer(1)).wait_send()

    def sum_copy(k):
        return remote(sum_out, sums_vmem.at[k], sum_send, sum_recv, other(k), me)

    def share_copy(part, k):
        return remote(
            give_ref.at[part, other(k)], share_ref.at[part, k],
            share_send, share_recv.at[part], other(k), me,
        )

    def strip_copy(part, k, owner):
        rows = padded_ref.at[part, pl.ds(1 + 2 * owner, 2), :, pl.ds(0, TILE)]
        return remote(rows, rows, strip_send, strip_recv.at[part], other(k), me)

    def edge_copy(part, side, k):
        return remote(
            edge_out.at[part], edge_ref.at[part, side, k],
            edge_send, edge_recv.at[part], other(k), neighbour(side),
        )

    def pack(part, to, target, at):
        rows = pl.ds(pl.multiple_of(part * CH, 16), CH)
        for c in range(CAP):
            target[part, at, c] = science_ref[source_ref[0, to * CAP + c], rows, :]

    @pl.loop(1, OWNERS)
    def _(k):
        coef_copy(k, peer(k), me).start()
        label_copy(k, peer(k), me).start()

    def send_tiles(batch):
        part = batch // GROUPS

        @pl.loop(1, GATHERED + 1)
        def _(n):
            k = (batch % GROUPS) * GATHERED + n
            pack(part, peer(k), outgoing_ref, peer(k))
            tile_copy(part, k, peer(k), me).start()

    @pl.loop(0, AHEAD)
    def _(batch):
        send_tiles(batch)

    @pl.loop(0, CHUNKS)
    def _(part):
        pack(part, me, arrived_ref, me)

    labels_vmem[me] = label_out[...]
    coefs_vmem[me] = coef_out[me]

    arrive(coefs_vmem.at[pl.ds(0, OWNERS - 1)], coef_recv)

    coef_local = pltpu.make_async_copy(coefs_vmem, coef_ref, local_sem.at[5])
    coef_local.start()
    row = coefs_vmem[0]
    for at in range(1, OWNERS):
        row = row + coefs_vmem[at]
    sum_out[...] = row

    @pl.loop(1, VISITORS)
    def _(k):
        sum_copy(k).start()

    across_copy.wait()
    down_copy.wait()
    build_weights(me, kw_ref, across_ref, w_ref)
    blank = jnp.zeros((CH, 2 * TILE), jnp.bfloat16)
    for part in range(CHUNKS):
        padded_ref[part, 0] = blank
        padded_ref[part, PT + 1] = blank
    for copy in prior_copies:
        copy.wait()
    coef_local.wait()

    def add_slots(part, at, fresh):
        tiles = [arrived_ref[part, at, c].astype(jnp.float32) for c in range(CAP)]
        for t in range(PT):
            value = None if fresh else acc_ref[t]
            for c in range(CAP):
                term = coef_ref[at, 0, t * CAP + c] * tiles[c]
                value = term if value is None else value + term
            acc_ref[t] = value

    def gather(part):
        add_slots(part, me, True)

        @pl.loop(0, (OWNERS - 1) // GATHERED)
        def _(group):
            arrive(arrived_ref.at[part, pl.ds(0, GATHERED)], tile_recv.at[part, group])
            batch = part * GROUPS + group + AHEAD

            @pl.when(batch < CHUNKS * GROUPS)
            def _():
                send_tiles(batch)

            @pl.loop(1, GATHERED + 1)
            def _(k):
                add_slots(part, origin(group * GATHERED + k), False)

        for to in range(VISITORS):
            for n in range(2):
                give_ref[part, to, n] = acc_ref[2 * to + n].astype(jnp.bfloat16)

        @pl.loop(1, VISITORS)
        def _(k):
            share_copy(part, k).start()

        own_ref[part] = acc_ref[pl.ds(own * 2, 2)]

    def finish(part):
        arrive(share_ref.at[part, pl.ds(1, VISITORS - 1)], share_recv.at[part])

        total_row = sum_out[...]
        for k in range(1, VISITORS):
            total_row = total_row + sums_vmem[k]
        spot = lax.broadcasted_iota(jnp.int32, (HALO, TILE), 1)
        packed = jnp.zeros((HALO, TILE), jnp.float32)
        for n in range(2):
            total = own_ref[part, n]
            for k in range(1, VISITORS):
                total = total + share_ref[part, k, n].astype(jnp.float32)
            weight_sum = jnp.sum(
                jnp.where(lane >> 2 == own * 2 + n, total_row, 0.0), axis=1, keepdims=True
            )
            rows = pl.ds(pl.multiple_of(n * TILE + part * CH, 16), CH)
            weight = prior_vmem[1, rows, :]
            template = (weight * prior_vmem[0, rows, :] + total) / (weight + weight_sum)
            template = template.astype(jnp.bfloat16)
            padded_ref[part, 1 + own * 2 + n, :, :TILE] = template
            wide = template.astype(jnp.float32)
            for h in range(2):
                g = 2 * n + h
                moved = pltpu.roll(
                    wide[h * HALO : (h + 1) * HALO], (2 * HALO * g + HALO) % TILE, 1
                )
                packed = jnp.where(spot >> 5 == g, moved, packed)
        edge_out[part] = packed.astype(jnp.bfloat16)

        @pl.loop(0, VISITORS)
        def _(k):
            for side in range(2):
                edge_copy(part, side, k).start()

        @pl.loop(1, VISITORS)
        def _(k):
            strip_copy(part, k, own).start()

    def wait_strips(part):
        spot = lax.broadcasted_iota(jnp.int32, (HALO, TILE), 1)

        arrive(
            padded_ref.at[part, pl.ds(1, PT - 2), :, pl.ds(0, TILE)], strip_recv.at[part]
        )
        arrive(edge_ref.at[part], edge_recv.at[part])

        @pl.loop(0, VISITORS)
        def _(k):
            left = jnp.where(me > 0, edge_ref[part, 0, k].astype(jnp.float32), 0.0)
            right = jnp.where(me < OWNERS - 1, edge_ref[part, 1, k].astype(jnp.float32), 0.0)
            both = jnp.where(spot & (2 * HALO - 1) < HALO, left, right)
            for g in range(4):
                moved = pltpu.roll(both, (TILE - 2 * HALO * g) % TILE, 1) if g else both
                moved = jnp.where(spot < 2 * HALO, moved, 0.0).astype(jnp.bfloat16)
                n, h = g // 2, g % 2
                padded_ref[
                    part, 1 + earlier(k) * 2 + n, h * HALO : (h + 1) * HALO, TILE:
                ] = moved

    label_local = pltpu.make_async_copy(labels_vmem, labels_ref, local_sem.at[6])

    @pl.loop(0, CHUNKS - 1)
    def _(step):
        gather(step)

        @pl.when(step == 1)
        def _():
            arrive(labels_vmem.at[pl.ds(0, OWNERS - 1)], label_recv)
            label_local.start()
            label_local.wait()

        @pl.when(step == 0)
        def _():
            arrive(sums_vmem.at[pl.ds(1, VISITORS - 1)], sum_recv)

        @pl.when(step > 0)
        def _():
            finish(step - 1)

        @pl.when(step > 1)
        def _():
            wait_strips(step - 2)

    finish(CHUNKS - 2)
    gather(CHUNKS - 1)

    @pl.loop(CHUNKS - 3, CHUNKS - 1)
    def _(part):
        wait_strips(part)

    @pl.loop(0, CHUNKS)
    def _(step):
        part = lax.rem(step + 1, CHUNKS)

        @pl.when(step == 1)
        def _():
            wait_strips(CHUNKS - 1)

        match_chunk(part, padded_ref, down_ref, w_ref, columns_ref, matched_ref)

        @pl.when(step == 0)
        def _():
            finish(CHUNKS - 1)

        @pl.loop(1, OWNERS)
        def _(k):
            to = peer(k)
            for c in range(CAP):
                back_out[part, to, c] = matched_ref[labels_ref[to, 0, me * CAP + c]]
            for q in range(CHUNKS):

                @pl.when(part == q)
                def _():
                    back_copy(q, k, to, me).start()

        for q in range(CHUNKS):

            @pl.when(part == q)
            def _():
                for c in range(CAP):
                    returned[q][me, c] = matched_ref[labels_ref[me, 0, me * CAP + c]]

    written = []
    for step in range(CHUNKS):
        part = (step + 1) % CHUNKS
        rows = pl.ds(part * CH, CH)
        arrive(returned[part].at[pl.ds(0, OWNERS - 1)], back_recv.at[part])

        @pl.loop(0, slots)
        def _(n):
            at = position_ref[n]
            matched = returned[part][at >> 2, at & (CAP - 1)].astype(jnp.float32)
            value = science_ref[n, rows, :].astype(jnp.float32) - matched
            keep = valid_ref[n // PT, n % PT].astype(jnp.float32)
            out_vmem[n, rows, :] = (value * keep).astype(jnp.bfloat16)

        copy = pltpu.make_async_copy(
            out_vmem.at[:, rows, :], out_ref.at[:, rows, :], local_sem.at[10 + part]
        )
        copy.start()
        written.append(copy)

    leave(coefs_vmem.at[pl.ds(0, OWNERS - 1)], coef_send)
    leave(labels_vmem.at[pl.ds(0, OWNERS - 1)], label_send)
    leave(sums_vmem.at[pl.ds(1, VISITORS - 1)], sum_send)
    leave(give_ref.at[:, pl.ds(0, VISITORS - 1)], share_send)
    leave(padded_ref.at[:, pl.ds(1, PT - 2), :, pl.ds(0, TILE)], strip_send)
    leave(edge_ref, edge_send)
    leave(outgoing_ref.at[:, pl.ds(0, OWNERS - 1)], tile_send)
    leave(back_out.at[:, pl.ds(0, OWNERS - 1)], back_send)
    for copy in written:
        copy.wait()


def body(science, tile_ids, valid, weights, kernel_weight_terms, prior_template, prior_weight):
    slots = tile_ids.size
    across, down = band_constants()
    vmem = pl.BlockSpec(memory_space=pltpu.VMEM)
    smem = pl.BlockSpec(memory_space=pltpu.SMEM)
    hbm = pl.BlockSpec(memory_space=pl.ANY)
    dma = pltpu.SemaphoreType.DMA
    f32, bf16, i32 = jnp.float32, jnp.bfloat16, jnp.int32
    result = pl.pallas_call(
        kernel,
        out_shape=jax.ShapeDtypeStruct((slots, TILE, TILE), jnp.bfloat16),
        in_specs=[smem, smem, vmem, vmem, hbm, hbm, hbm, hbm, hbm],
        out_specs=hbm,
        scratch_shapes=[
            pltpu.VMEM((slots, TILE, TILE), bf16),
            pltpu.VMEM((slots, TILE, TILE), bf16),
            pltpu.VMEM(across.shape, bf16),
            pltpu.VMEM(down.shape, bf16),
            pltpu.VMEM((DEEP, GROUP), bf16),
            pltpu.VMEM((PT * CH, DEEP), bf16),
            pltpu.VMEM((CHUNKS, PT + 2, CH, 2 * TILE), bf16),
            pltpu.VMEM((VIS * PT, CH, TILE), bf16),
            pltpu.VMEM((CHUNKS, OWNERS, CAP, CH, TILE), bf16),
            pltpu.VMEM((CHUNKS, OWNERS, CAP, CH, TILE), bf16),
            pltpu.VMEM((OWNERS, CAP, CH, TILE), bf16),
            pltpu.VMEM((OWNERS, CAP, CH, TILE), bf16),
            pltpu.VMEM((OWNERS, CAP, CH, TILE), bf16),
            pltpu.VMEM((OWNERS, CAP, CH, TILE), bf16),
            pltpu.VMEM((CHUNKS, OWNERS, CAP, CH, TILE), bf16),
            pltpu.VMEM((PT, CH, TILE), f32),
            pltpu.VMEM((CHUNKS, 2, CH, TILE), f32),
            pltpu.VMEM((CHUNKS, VISITORS, 2, CH, TILE), bf16),
            pltpu.VMEM((CHUNKS, VISITORS, 2, CH, TILE), bf16),
            pltpu.VMEM((CHUNKS, HALO, TILE), bf16),
            pltpu.VMEM((CHUNKS, 2, VISITORS, HALO, TILE), bf16),
            pltpu.VMEM((2, 2 * TILE, TILE), f32),
            pltpu.VMEM(weights.shape, f32),
            pltpu.VMEM((NPOLY, VIS, NBASIS), f32),
            pltpu.VMEM((1, TILE), i32),
            pltpu.VMEM((1, TILE), i32),
            pltpu.VMEM((OWNERS, 1, TILE), i32),
            pltpu.VMEM((OWNERS, 1, TILE), f32),
            pltpu.VMEM((OWNERS, 1, TILE), f32),
            pltpu.VMEM((1, TILE), f32),
            pltpu.VMEM((VISITORS, 1, TILE), f32),
            pltpu.SMEM(weights.shape, f32),
            pltpu.SMEM((NPOLY, VIS, NBASIS), f32),
            pltpu.SMEM((1, TILE), i32),
            pltpu.SMEM((slots,), i32),
            pltpu.SMEM((OWNERS, 1, TILE), i32),
            pltpu.SMEM((OWNERS, 1, TILE), f32),
            dma((10 + CHUNKS,)),
            dma(()),
            dma(()),
            dma(()),
            dma(()),
            dma(()),
            dma((CHUNKS, (OWNERS - 1) // GATHERED)),
            dma(()),
            dma((CHUNKS,)),
            dma(()),
            dma((CHUNKS,)),
            dma(()),
            dma((CHUNKS,)),
            dma(()),
            dma(()),
            dma(()),
            dma((CHUNKS,)),
        ],
        compiler_params=pltpu.CompilerParams(
            vmem_limit_bytes=56 << 20, collective_id=0, has_side_effects=True
        ),
    )(
        tile_ids,
        valid,
        weights,
        jnp.transpose(kernel_weight_terms, (1, 0, 2)),
        science.reshape(slots, TILE, TILE),
        prior_template,
        prior_weight,
        jnp.asarray(across),
        jnp.asarray(down),
    )
    return result.reshape(science.shape)


def solution(mesh):
    placed = (
        P("visit", "patch", None, None),
        P("visit", "patch"),
        P("visit", "patch"),
        P("visit", "patch"),
        P("visit", None, None),
        P(None, "patch"),
        P(None, "patch"),
    )
    return jax.shard_map(
        body, mesh=mesh, in_specs=placed, out_specs=P("visit", "patch", None, None), check_vma=False
    )
```

```python
import jax
import jax.numpy as jnp
import ml_dtypes
import numpy as np
from jax import lax
from jax.experimental import pallas as pl
from jax.experimental.pallas import tpu as pltpu
from jax.sharding import PartitionSpec as P

TILE = 128
KHALF = 15
HALO = 16
SPAN = TILE + 2 * HALO
SIGMAS = (1.5, 3.0, 5.0, 7.0)
DEGREES = (4, 2, 1, 0)
NPROF = 11
NBASIS = 25
NPOLY = 6
PT = 16
SKY = 2048
VIS = 2
GROUP = 3 * VIS * TILE
CH = 32
CHUNKS = TILE // CH
MAIN = NPROF * TILE
DEEP = MAIN + 3 * TILE
OWNERS = 16
VISITORS = 8
CAP = 4
GATHERED = 3
GROUPS = (OWNERS - 1) // GATHERED
AHEAD = 7
MESH = pl.DeviceIdType.MESH


def profile_table():
    u = np.arange(-KHALF, KHALF + 1, dtype=np.float32)
    rows = []
    for sigma, degree in zip(SIGMAS, DEGREES):
        scaled = u / np.float32(sigma)
        envelope = np.exp(np.float32(-0.5) * scaled * scaled)
        for power in range(degree + 1):
            shaped = envelope * scaled**power
            rows.append(shaped / np.sum(np.abs(shaped)))
    return np.stack(rows).astype(np.float32)


def band_constants():
    profiles = profile_table()
    target = np.arange(TILE)

    def band(source):
        taps = source[:, None] - target[None, :] + KHALF
        inside = (taps >= 0) & (taps <= 2 * KHALF)
        return np.where(inside[None], profiles[:, np.clip(taps, 0, 2 * KHALF)], 0.0)

    columns = np.concatenate(
        [np.arange(TILE), np.arange(-HALO, 0), np.arange(TILE, TILE + HALO)]
    )
    across = band(columns).astype(ml_dtypes.bfloat16)
    down = band(np.arange(-HALO, CH + HALO))[:, :, :CH].transpose(0, 2, 1)
    down = down.reshape(NPROF * CH, CH + 2 * HALO).astype(ml_dtypes.bfloat16)
    return across, down


def basis_order():
    order, start = [], 0
    for degree in DEGREES:
        for j in range(degree + 1):
            order.append((start + j, [start + i for i in range(degree - j + 1)]))
        start += degree + 1
    return order


def build_weights(strip, kw_ref, across_ref, w_ref):
    lane = lax.broadcasted_iota(jnp.int32, (1, TILE), 1) + strip * TILE
    x = (lane.astype(jnp.float32) + 0.5) / SKY * 2.0 - 1.0
    xx = x * x
    unused = MAIN + NPROF * 2 * HALO
    w_ref[unused:, :] = jnp.zeros((DEEP - unused, GROUP), jnp.bfloat16)
    k = 0
    for j, sources in basis_order():
        for v in range(VIS):
            sums = [None, None, None]
            for n, source in enumerate(sources):
                c = [kw_ref[m, v, k + n] for m in range(NPOLY)]
                rows = (c[0] + c[1] * x + c[3] * xx, c[2] + c[4] * x, c[5])
                image = across_ref[source].astype(jnp.float32)
                for b in range(3):
                    term = rows[b] * image
                    sums[b] = term if sums[b] is None else sums[b] + term
            for b in range(3):
                at = (b * VIS + v) * TILE
                value = sums[b].astype(jnp.bfloat16)
                halo = MAIN + j * 2 * HALO
                w_ref[j * TILE : (j + 1) * TILE, at : at + TILE] = value[:TILE]
                w_ref[halo : halo + 2 * HALO, at : at + TILE] = value[TILE:]
        k += len(sources)


def match_chunk(part, padded_ref, down_ref, w_ref, columns_ref, matched_ref):
    first = (part == 0).astype(jnp.int32)
    last = (part == CHUNKS - 1).astype(jnp.int32)
    before = lax.rem(part + CHUNKS - 1, CHUNKS)
    after = lax.rem(part + 1, CHUNKS)

    @pl.loop(0, PT, unroll=True)
    def _(tile):
        rows = pl.ds(pl.multiple_of(tile * CH, 16), CH)
        window = jnp.concatenate(
            [
                padded_ref[before, tile + 1 - first, CH - HALO :, :],
                padded_ref[part, tile + 1],
                padded_ref[after, tile + 1 + last, :HALO, :],
            ],
            axis=0,
        )
        both = jnp.dot(down_ref[...], window, preferred_element_type=jnp.float32)
        for group in range(3):
            total = None
            for q in range(min(4, NPROF - 4 * group)):
                j = 4 * group + q
                piece = both[j * CH : (j + 1) * CH]
                columns_ref[rows, j * TILE : (j + 1) * TILE] = piece[:, :TILE].astype(jnp.bfloat16)
                side = piece[:, TILE:]
                side = pltpu.roll(side, 2 * HALO * q, 1) if q else side
                total = side if total is None else total + side
            at = MAIN + group * TILE
            columns_ref[rows, at : at + TILE] = total.astype(jnp.bfloat16)

    half = VIS * TILE
    line = lax.broadcasted_iota(jnp.int32, (PT * CH, 1), 0)
    y = ((line >> 5) * TILE + part * CH + (line & (CH - 1))).astype(jnp.float32)
    y = (y + 0.5) / SKY * 2.0 - 1.0
    total = jnp.zeros((PT * CH, half), jnp.float32)
    for power, factor in enumerate((None, y, y * y)):
        term = jnp.dot(
            columns_ref[...],
            w_ref[:, power * half : (power + 1) * half],
            preferred_element_type=jnp.float32,
        )
        total = total + (term if factor is None else factor * term)
    total = total.astype(jnp.bfloat16)
    for v in range(VIS):
        for tile in range(PT):
            matched_ref[v * PT + tile] = total[
                tile * CH : (tile + 1) * CH, v * TILE : (v + 1) * TILE
            ]


def remote(src, dst, send, recv, visit, patch):
    return pltpu.make_async_remote_copy(
        src_ref=src,
        dst_ref=dst,
        send_sem=send,
        recv_sem=recv,
        device_id={"visit": visit, "patch": patch},
        device_id_type=MESH,
    )


def kernel(
    ids_ref, valid_ref, weights_ref, terms_ref, science_hbm,
    prior_ref, prior_weight_ref, across_hbm, down_hbm, out_ref,
    out_vmem, science_ref, across_ref, down_ref,
    w_ref, columns_ref, padded_ref, matched_ref, outgoing_ref, arrived_ref,
    back_0, back_1, back_2, back_3,
    back_out, acc_ref, own_ref, give_ref, share_ref, edge_out, edge_ref, prior_vmem,
    slot_weight_vmem, terms_vmem, source_vmem, label_out, labels_vmem, coef_out, coefs_vmem,
    sum_out, sums_vmem,
    slot_weight_ref, kw_ref, source_ref, position_ref, labels_ref, coef_ref,
    local_sem, label_send, label_recv, coef_send, coef_recv, tile_send, tile_recv,
    share_send, share_recv, strip_send, strip_recv, edge_send, edge_recv,
    sum_send, sum_recv, back_send, back_recv,
):
    visit = lax.axis_index("visit")
    me = lax.axis_index("patch")
    own = visit
    returned = (back_0, back_1, back_2, back_3)
    slots = VIS * PT

    def peer(k):
        return lax.rem(me + k, OWNERS)

    def origin(k):
        return lax.rem(me + OWNERS - k, OWNERS)

    def other(k):
        return lax.rem(visit + k, VISITORS)

    def earlier(k):
        return lax.rem(visit + VISITORS - k, VISITORS)

    def neighbour(side):
        return peer(1) if side == 0 else origin(1)

    science_copy = pltpu.make_async_copy(science_hbm, science_ref, local_sem.at[7])
    across_copy = pltpu.make_async_copy(across_hbm, across_ref, local_sem.at[8])
    down_copy = pltpu.make_async_copy(down_hbm, down_ref, local_sem.at[9])
    science_copy.start()
    barrier = pltpu.get_barrier_semaphore()

    def greet(to_visit, to_patch):
        pl.semaphore_signal(
            barrier, inc=1, device_id={"visit": to_visit, "patch": to_patch}, device_id_type=MESH
        )

    @pl.loop(1, OWNERS)
    def _(k):
        greet(visit, peer(k))

    @pl.loop(1, VISITORS)
    def _(k):
        greet(other(k), me)
        greet(other(k), peer(1))
        greet(other(k), origin(1))

    prior_copies = [
        pltpu.make_async_copy(
            ref.at[pl.ds(pl.multiple_of(own * 256, 256), 256), :],
            prior_vmem.at[n],
            local_sem.at[n],
        )
        for n, ref in enumerate((prior_ref, prior_weight_ref))
    ]
    for copy in prior_copies:
        copy.start()
    across_copy.start()
    down_copy.start()
    slot_weight_vmem[...] = weights_ref[...].astype(jnp.float32)
    terms_vmem[...] = terms_ref[...].astype(jnp.float32)
    weight_copy = pltpu.make_async_copy(slot_weight_vmem, slot_weight_ref, local_sem.at[2])
    terms_copy = pltpu.make_async_copy(terms_vmem, kw_ref, local_sem.at[3])
    weight_copy.start()
    terms_copy.start()

    ids = [ids_ref[n // PT, n % PT] for n in range(slots)]
    strips = [value >> 4 for value in ids]
    tiles = [value & (PT - 1) for value in ids]
    for n in range(slots):
        rank = 0
        for m in range(n):
            rank = rank + jnp.where(strips[m] == strips[n], 1, 0)
        position_ref[n] = strips[n] * CAP + rank

    lane = lax.broadcasted_iota(jnp.int32, (1, TILE), 1)
    source = jnp.zeros((1, TILE), jnp.int32)
    label = jnp.zeros((1, TILE), jnp.int32)
    for n in range(slots):
        here = lane == position_ref[n]
        source = jnp.where(here, n, source)
        label = jnp.where(here, n // PT * PT + tiles[n], label)
    source_vmem[...] = source
    label_out[...] = label
    source_copy = pltpu.make_async_copy(source_vmem, source_ref, local_sem.at[4])
    source_copy.start()
    weight_copy.wait()
    owner_row = lax.broadcasted_iota(jnp.int32, (OWNERS, TILE), 0)
    entry = lax.broadcasted_iota(jnp.int32, (OWNERS, TILE), 1)
    coefs = jnp.zeros((OWNERS, TILE), jnp.float32)
    for n in range(slots):
        v, s = n // PT, n % PT
        at = position_ref[n]
        here = (owner_row == at >> 2) & (entry == tiles[n] * CAP + (at & (CAP - 1)))
        weight = slot_weight_ref[v, s] * valid_ref[v, s].astype(jnp.float32)
        coefs = jnp.where(here, weight, coefs)
    for to in range(OWNERS):
        coef_out[to] = coefs[to : to + 1]
    source_copy.wait()
    terms_copy.wait()
    science_copy.wait()

    pl.semaphore_wait(barrier, OWNERS - 1 + 3 * (VISITORS - 1))

    def coef_copy(k, to, slot):
        return remote(
            coef_out.at[to], coefs_vmem.at[slot], coef_send, coef_recv, visit, to
        )

    def label_copy(k, to, slot):
        return remote(
            label_out, labels_vmem.at[slot], label_send, label_recv, visit, to
        )

    def tile_copy(part, k, to, slot):
        return remote(
            outgoing_ref.at[part, to], arrived_ref.at[part, slot],
            tile_send, tile_recv.at[part, (k - 1) // GATHERED], visit, to,
        )

    def back_copy(part, k, to, slot):
        return remote(
            back_out.at[part, to], returned[part].at[slot],
            back_send, back_recv.at[part], visit, to,
        )

    def arrive(block, semaphore):
        remote(block, block, semaphore, semaphore, visit, peer(1)).wait_recv()

    def leave(block, semaphore):
        remote(block, block, semaphore, semaphore, visit, peer(1)).wait_send()

    def sum_copy(k):
        return remote(sum_out, sums_vmem.at[k], sum_send, sum_recv, other(k), me)

    def share_copy(part, k):
        return remote(
            give_ref.at[part, other(k)], share_ref.at[part, k],
            share_send, share_recv.at[part], other(k), me,
        )

    def strip_copy(part, k, owner):
        rows = padded_ref.at[part, pl.ds(1 + 2 * owner, 2), :, pl.ds(0, TILE)]
        return remote(rows, rows, strip_send, strip_recv.at[part], other(k), me)

    def edge_copy(part, side, k):
        return remote(
            edge_out.at[part], edge_ref.at[part, side, k],
            edge_send, edge_recv.at[part], other(k), neighbour(side),
        )

    def pack(part, to, target, at):
        rows = pl.ds(pl.multiple_of(part * CH, 16), CH)
        for c in range(CAP):
            target[part, at, c] = science_ref[source_ref[0, to * CAP + c], rows, :]

    @pl.loop(1, OWNERS)
    def _(k):
        coef_copy(k, peer(k), me).start()
        label_copy(k, peer(k), me).start()

    def send_tiles(batch):
        part = batch // GROUPS

        @pl.loop(1, GATHERED + 1)
        def _(n):
            k = (batch % GROUPS) * GATHERED + n
            pack(part, peer(k), outgoing_ref, peer(k))
            tile_copy(part, k, peer(k), me).start()

    @pl.loop(0, AHEAD)
    def _(batch):
        send_tiles(batch)

    @pl.loop(0, CHUNKS)
    def _(part):
        pack(part, me, arrived_ref, me)

    labels_vmem[me] = label_out[...]
    coefs_vmem[me] = coef_out[me]

    arrive(coefs_vmem.at[pl.ds(0, OWNERS - 1)], coef_recv)

    coef_local = pltpu.make_async_copy(coefs_vmem, coef_ref, local_sem.at[5])
    coef_local.start()
    row = coefs_vmem[0]
    for at in range(1, OWNERS):
        row = row + coefs_vmem[at]
    sum_out[...] = row

    @pl.loop(1, VISITORS)
    def _(k):
        sum_copy(k).start()

    across_copy.wait()
    down_copy.wait()
    build_weights(me, kw_ref, across_ref, w_ref)
    blank = jnp.zeros((CH, 2 * TILE), jnp.bfloat16)
    for part in range(CHUNKS):
        padded_ref[part, 0] = blank
        padded_ref[part, PT + 1] = blank
    for copy in prior_copies:
        copy.wait()
    coef_local.wait()

    def add_slots(part, at, fresh):
        tiles = [arrived_ref[part, at, c].astype(jnp.float32) for c in range(CAP)]
        for t in range(PT):
            value = None if fresh else acc_ref[t]
            for c in range(CAP):
                term = coef_ref[at, 0, t * CAP + c] * tiles[c]
                value = term if value is None else value + term
            acc_ref[t] = value

    def gather(part):
        add_slots(part, me, True)

        @pl.loop(0, (OWNERS - 1) // GATHERED)
        def _(group):
            arrive(arrived_ref.at[part, pl.ds(0, GATHERED)], tile_recv.at[part, group])
            batch = part * GROUPS + group + AHEAD

            @pl.when(batch < CHUNKS * GROUPS)
            def _():
                send_tiles(batch)

            @pl.loop(1, GATHERED + 1)
            def _(k):
                add_slots(part, origin(group * GATHERED + k), False)

        for to in range(VISITORS):
            for n in range(2):
                give_ref[part, to, n] = acc_ref[2 * to + n].astype(jnp.bfloat16)

        @pl.loop(1, VISITORS)
        def _(k):
            share_copy(part, k).start()

        own_ref[part] = acc_ref[pl.ds(own * 2, 2)]

    def finish(part):
        arrive(share_ref.at[part, pl.ds(1, VISITORS - 1)], share_recv.at[part])

        total_row = sum_out[...]
        for k in range(1, VISITORS):
            total_row = total_row + sums_vmem[k]
        spot = lax.broadcasted_iota(jnp.int32, (HALO, TILE), 1)
        packed = jnp.zeros((HALO, TILE), jnp.float32)
        for n in range(2):
            total = own_ref[part, n]
            for k in range(1, VISITORS):
                total = total + share_ref[part, k, n].astype(jnp.float32)
            weight_sum = jnp.sum(
                jnp.where(lane >> 2 == own * 2 + n, total_row, 0.0), axis=1, keepdims=True
            )
            rows = pl.ds(pl.multiple_of(n * TILE + part * CH, 16), CH)
            weight = prior_vmem[1, rows, :]
            template = (weight * prior_vmem[0, rows, :] + total) / (weight + weight_sum)
            template = template.astype(jnp.bfloat16)
            padded_ref[part, 1 + own * 2 + n, :, :TILE] = template
            wide = template.astype(jnp.float32)
            for h in range(2):
                g = 2 * n + h
                moved = pltpu.roll(
                    wide[h * HALO : (h + 1) * HALO], (2 * HALO * g + HALO) % TILE, 1
                )
                packed = jnp.where(spot >> 5 == g, moved, packed)
        edge_out[part] = packed.astype(jnp.bfloat16)

        @pl.loop(0, VISITORS)
        def _(k):
            for side in range(2):
                edge_copy(part, side, k).start()

        @pl.loop(1, VISITORS)
        def _(k):
            strip_copy(part, k, own).start()

    def wait_strips(part):
        spot = lax.broadcasted_iota(jnp.int32, (HALO, TILE), 1)

        arrive(
            padded_ref.at[part, pl.ds(1, PT - 2), :, pl.ds(0, TILE)], strip_recv.at[part]
        )
        arrive(edge_ref.at[part], edge_recv.at[part])

        @pl.loop(0, VISITORS)
        def _(k):
            left = jnp.where(me > 0, edge_ref[part, 0, k].astype(jnp.float32), 0.0)
            right = jnp.where(me < OWNERS - 1, edge_ref[part, 1, k].astype(jnp.float32), 0.0)
            both = jnp.where(spot & (2 * HALO - 1) < HALO, left, right)
            for g in range(4):
                moved = pltpu.roll(both, (TILE - 2 * HALO * g) % TILE, 1) if g else both
                moved = jnp.where(spot < 2 * HALO, moved, 0.0).astype(jnp.bfloat16)
                n, h = g // 2, g % 2
                padded_ref[
                    part, 1 + earlier(k) * 2 + n, h * HALO : (h + 1) * HALO, TILE:
                ] = moved

    label_local = pltpu.make_async_copy(labels_vmem, labels_ref, local_sem.at[6])

    @pl.loop(0, CHUNKS - 1)
    def _(step):
        gather(step)

        @pl.when(step == 1)
        def _():
            arrive(labels_vmem.at[pl.ds(0, OWNERS - 1)], label_recv)
            label_local.start()
            label_local.wait()

        @pl.when(step == 0)
        def _():
            arrive(sums_vmem.at[pl.ds(1, VISITORS - 1)], sum_recv)

        @pl.when(step > 0)
        def _():
            finish(step - 1)

        @pl.when(step > 1)
        def _():
            wait_strips(step - 2)

    finish(CHUNKS - 2)
    wait_strips(CHUNKS - 3)
    gather(CHUNKS - 1)
    wait_strips(CHUNKS - 2)

    @pl.loop(0, CHUNKS)
    def _(step):
        part = lax.rem(step + 1, CHUNKS)

        @pl.when(step == 1)
        def _():
            wait_strips(CHUNKS - 1)

        match_chunk(part, padded_ref, down_ref, w_ref, columns_ref, matched_ref)

        @pl.when(step == 0)
        def _():
            finish(CHUNKS - 1)

        for q in range(CHUNKS):

            @pl.when(part == q)
            def _():
                @pl.loop(1, OWNERS)
                def _(k):
                    to = peer(k)
                    for c in range(CAP):
                        back_out[q, to, c] = matched_ref[labels_ref[to, 0, me * CAP + c]]
                    back_copy(q, k, to, me).start()

                for c in range(CAP):
                    returned[q][me, c] = matched_ref[labels_ref[me, 0, me * CAP + c]]

    written = []
    for step in range(CHUNKS):
        part = (step + 1) % CHUNKS
        rows = pl.ds(part * CH, CH)
        arrive(returned[part].at[pl.ds(0, OWNERS - 1)], back_recv.at[part])

        @pl.loop(0, slots)
        def _(n):
            at = position_ref[n]
            matched = returned[part][at >> 2, at & (CAP - 1)].astype(jnp.float32)
            value = science_ref[n, rows, :].astype(jnp.float32) - matched
            keep = valid_ref[n // PT, n % PT].astype(jnp.float32)
            out_vmem[n, rows, :] = (value * keep).astype(jnp.bfloat16)

        copy = pltpu.make_async_copy(
            out_vmem.at[:, rows, :], out_ref.at[:, rows, :], local_sem.at[10 + part]
        )
        copy.start()
        written.append(copy)

    leave(coefs_vmem.at[pl.ds(0, OWNERS - 1)], coef_send)
    leave(labels_vmem.at[pl.ds(0, OWNERS - 1)], label_send)
    leave(sums_vmem.at[pl.ds(1, VISITORS - 1)], sum_send)
    leave(give_ref.at[:, pl.ds(0, VISITORS - 1)], share_send)
    leave(padded_ref.at[:, pl.ds(1, PT - 2), :, pl.ds(0, TILE)], strip_send)
    leave(edge_ref, edge_send)
    leave(outgoing_ref.at[:, pl.ds(0, OWNERS - 1)], tile_send)
    leave(back_out.at[:, pl.ds(0, OWNERS - 1)], back_send)
    for copy in written:
        copy.wait()


def body(science, tile_ids, valid, weights, kernel_weight_terms, prior_template, prior_weight):
    slots = tile_ids.size
    across, down = band_constants()
    vmem = pl.BlockSpec(memory_space=pltpu.VMEM)
    smem = pl.BlockSpec(memory_space=pltpu.SMEM)
    hbm = pl.BlockSpec(memory_space=pl.ANY)
    dma = pltpu.SemaphoreType.DMA
    f32, bf16, i32 = jnp.float32, jnp.bfloat16, jnp.int32
    result = pl.pallas_call(
        kernel,
        out_shape=jax.ShapeDtypeStruct((slots, TILE, TILE), jnp.bfloat16),
        in_specs=[smem, smem, vmem, vmem, hbm, hbm, hbm, hbm, hbm],
        out_specs=hbm,
        scratch_shapes=[
            pltpu.VMEM((slots, TILE, TILE), bf16),
            pltpu.VMEM((slots, TILE, TILE), bf16),
            pltpu.VMEM(across.shape, bf16),
            pltpu.VMEM(down.shape, bf16),
            pltpu.VMEM((DEEP, GROUP), bf16),
            pltpu.VMEM((PT * CH, DEEP), bf16),
            pltpu.VMEM((CHUNKS, PT + 2, CH, 2 * TILE), bf16),
            pltpu.VMEM((VIS * PT, CH, TILE), bf16),
            pltpu.VMEM((CHUNKS, OWNERS, CAP, CH, TILE), bf16),
            pltpu.VMEM((CHUNKS, OWNERS, CAP, CH, TILE), bf16),
            pltpu.VMEM((OWNERS, CAP, CH, TILE), bf16),
            pltpu.VMEM((OWNERS, CAP, CH, TILE), bf16),
            pltpu.VMEM((OWNERS, CAP, CH, TILE), bf16),
            pltpu.VMEM((OWNERS, CAP, CH, TILE), bf16),
            pltpu.VMEM((CHUNKS, OWNERS, CAP, CH, TILE), bf16),
            pltpu.VMEM((PT, CH, TILE), f32),
            pltpu.VMEM((CHUNKS, 2, CH, TILE), f32),
            pltpu.VMEM((CHUNKS, VISITORS, 2, CH, TILE), bf16),
            pltpu.VMEM((CHUNKS, VISITORS, 2, CH, TILE), bf16),
            pltpu.VMEM((CHUNKS, HALO, TILE), bf16),
            pltpu.VMEM((CHUNKS, 2, VISITORS, HALO, TILE), bf16),
            pltpu.VMEM((2, 2 * TILE, TILE), f32),
            pltpu.VMEM(weights.shape, f32),
            pltpu.VMEM((NPOLY, VIS, NBASIS), f32),
            pltpu.VMEM((1, TILE), i32),
            pltpu.VMEM((1, TILE), i32),
            pltpu.VMEM((OWNERS, 1, TILE), i32),
            pltpu.VMEM((OWNERS, 1, TILE), f32),
            pltpu.VMEM((OWNERS, 1, TILE), f32),
            pltpu.VMEM((1, TILE), f32),
            pltpu.VMEM((VISITORS, 1, TILE), f32),
            pltpu.SMEM(weights.shape, f32),
            pltpu.SMEM((NPOLY, VIS, NBASIS), f32),
            pltpu.SMEM((1, TILE), i32),
            pltpu.SMEM((slots,), i32),
            pltpu.SMEM((OWNERS, 1, TILE), i32),
            pltpu.SMEM((OWNERS, 1, TILE), f32),
            dma((10 + CHUNKS,)),
            dma(()),
            dma(()),
            dma(()),
            dma(()),
            dma(()),
            dma((CHUNKS, (OWNERS - 1) // GATHERED)),
            dma(()),
            dma((CHUNKS,)),
            dma(()),
            dma((CHUNKS,)),
            dma(()),
            dma((CHUNKS,)),
            dma(()),
            dma(()),
            dma(()),
            dma((CHUNKS,)),
        ],
        compiler_params=pltpu.CompilerParams(
            vmem_limit_bytes=56 << 20, collective_id=0, has_side_effects=True
        ),
    )(
        tile_ids,
        valid,
        weights,
        jnp.transpose(kernel_weight_terms, (1, 0, 2)),
        science.reshape(slots, TILE, TILE),
        prior_template,
        prior_weight,
        jnp.asarray(across),
        jnp.asarray(down),
    )
    return result.reshape(science.shape)


def solution(mesh):
    placed = (
        P("visit", "patch", None, None),
        P("visit", "patch"),
        P("visit", "patch"),
        P("visit", "patch"),
        P("visit", None, None),
        P(None, "patch"),
        P(None, "patch"),
    )
    return jax.shard_map(
        body, mesh=mesh, in_specs=placed, out_specs=P("visit", "patch", None, None), check_vma=False
    )
```
